512 devices in a mesh: tpl: 8 (over y, core), sta: 64 (over x, z).
Axes of the slice: x: 4, y: 4, z: 16, core: 2. Of those that a mesh axis runs over, the one named last changes fastest.
Arguments:
- samples: bfloat16 [1024, 3, 1152], P('sta', None, 'tpl'), may hold values from -6 to 6
- templates: bfloat16 [2048, 20, 3, 384], P(('tpl', 'sta')), may hold values from -6 to 6
- station_list: int32 [2048, 20], P(('tpl', 'sta')), may hold values from 0 to 1023, as said below
- station_count: int32 [2048], P(('tpl', 'sta')), may hold values from 10 to 20
- moveout: int32 [2048, 20], P(('tpl', 'sta')), may hold values from 0 to 287
- offsets: int32 [1024], replicated, may hold values from 0 to 95
Outputs:
- detection: float32 [2048, 384], P(('tpl', 'sta'))
The draws below stay inside these ranges and needn't reach their ends.
Inputs may be any that keep to these rules, and one draw needn't show every extreme that they name: `station_list`: A device's templates are 4 consecutive ones. Over all 20 entries of one device's templates, at most 2 fall in one block of 16 consecutive stations, and in every device some block holds exactly 2 of them, all among the first 2 entries of its first template. The entries of one template are distinct.
All inputs are finite; a program needn't handle non-finite values.
Results may differ from the reference program's by a relative error of at most 0.012.
Values may be sent and summed in bfloat16 or wider, within the bound.
A program may use at most 64 MiB of HBM per device.

```python
import math
import jax
import jax.numpy as jnp
from jax import lax

M = 384
CH = 3
KMAX = 20
STA_DEV = 16
TPL_DEV = 4
OWNERS = 64
CAP = 2
NSTA = 1024
NT = 2048
L = 1152
MOVE = 288
OFFS = 96


def draw_station_list(key, part):
    block_total = NT // TPL_DEV
    token_total = OWNERS * CAP
    positions = TPL_DEV * KMAX
    span_of = STA_DEV // CAP
    favoured = jax.random.randint(jax.random.fold_in(key, 7), (), 0, OWNERS)

    def one_block(block_key):
        shuffled = jax.random.permutation(block_key, token_total).astype(jnp.int32)
        rank_idx = jnp.arange(token_total, dtype=jnp.int32)
        scores = jnp.where(shuffled // CAP == favoured, shuffled % CAP, CAP + rank_idx)
        placed = shuffled[jnp.argsort(scores, stable=True)]
        chosen = placed[:positions]
        owner_of = chosen // CAP
        copy_of = chosen % CAP
        within = jax.random.randint(jax.random.fold_in(block_key, 3), (positions,), 0, span_of)
        return (owner_of * STA_DEV + copy_of * span_of + within).astype(jnp.int32)
    block_keys = jax.random.split(jax.random.fold_in(key, 11), block_total)
    return jax.vmap(one_block)(block_keys).reshape(NT, KMAX).astype(jnp.int32)


def with_ends(drawn, own_key, least, largest):
    extent = drawn.shape
    spot = [jax.random.randint(jax.random.fold_in(own_key, axis), (), 0, extent[axis]) for axis in range(len(extent))]
    drawn = drawn.at[tuple(spot)].set(least)
    longest = extent.index(max(extent))
    spot[longest] = (spot[longest] + 1) % extent[longest]
    return drawn.at[tuple(spot)].set(largest)


def block_scale(key, dims, cuts, least, top_value):
    loudness, own = 1.0, jax.random.fold_in(key, 6)
    for axis_at, blocks in cuts:
        heights = jnp.exp(jax.random.uniform(jax.random.fold_in(own, axis_at), (blocks,), jnp.float32, least / len(cuts), top_value / len(cuts)))
        loudness = loudness * jnp.repeat(heights, dims[axis_at] // blocks).reshape([-1 if axis == axis_at else 1 for axis in range(len(dims))])
    return loudness


def bell_draw(key, extent, deviation, reach, cuts=(), held_as=jnp.bfloat16):
    values = deviation * jax.random.normal(key, extent, jnp.float32)
    if cuts:
        values = values * block_scale(key, extent, cuts, -0.22, 0.18)
    return jnp.clip(values, -reach, reach).astype(held_as)


def setup_inputs(seed: int = 0) -> dict:
    key_list = jax.random.split(jax.random.key(seed), 7)
    return {
        "samples": bell_draw(key_list[0], (NSTA, CH, L), 1.0, 6.0, ((0, 64), (2, 8))),
        "templates": bell_draw(key_list[1], (NT, KMAX, CH, M), 1.0, 6.0, ((0, 512),)),
        "station_list": draw_station_list(jax.random.fold_in(key_list[6], 71), 0),
        "station_count": with_ends(jax.random.randint(key_list[3], (NT,), KMAX // 2, KMAX + 1), jax.random.fold_in(key_list[3], 1), KMAX // 2, KMAX).astype(jnp.int32),
        "moveout": with_ends(jax.random.randint(key_list[4], (NT, KMAX), 0, MOVE), jax.random.fold_in(key_list[4], 1), 0, MOVE - 1).astype(jnp.int32),
        "offsets": with_ends(jax.random.randint(key_list[5], (NSTA,), 0, OFFS), jax.random.fold_in(key_list[5], 1), 0, OFFS - 1).astype(jnp.int32),
    }


EPSILON = 1e-06

def tables(length, frame_len):
    row_idx = lax.broadcasted_iota(jnp.int32, (frame_len, frame_len), 0)
    col_idx = lax.broadcasted_iota(jnp.int32, (frame_len, frame_len), 1)
    angles = (row_idx * col_idx % frame_len).astype(jnp.float32) * (2.0 * math.pi / frame_len)
    cosine = jnp.cos(angles)
    sines = jnp.sin(angles)
    forward = jnp.concatenate([cosine, -sines], axis=1).astype(jnp.bfloat16)
    inverse = jnp.concatenate([cosine[:, :length], -sines[:, :length]], axis=0).astype(jnp.bfloat16)
    return (forward, inverse)

def station_blocks(series, length):
    block_count = series.shape[-1] // length - 1
    pieces = series.reshape(series.shape[:-1] + (block_count + 1, length))
    return jnp.concatenate([pieces[..., :-1, :], pieces[..., 1:, :]], axis=-1)

def spectra_of(blocks, forward):
    flat_rows = blocks.reshape(-1, blocks.shape[-1])
    result = jnp.dot(flat_rows, forward, preferred_element_type=jnp.float32).astype(jnp.bfloat16)
    return result.reshape(blocks.shape[:-1] + (forward.shape[1],))

def energy_of(blocks, length):
    squares_f = blocks.astype(jnp.float32) ** 2
    running = jnp.cumsum(squares_f, axis=-1)
    padded = jnp.concatenate([jnp.zeros(running.shape[:-1] + (1,), jnp.float32), running], axis=-1)
    windowed = padded[..., length:2 * length] - padded[..., :length]
    return windowed.reshape(blocks.shape[:-2] + (blocks.shape[-2] * length,))

def correlate(spectra, tmpl_spec, energy, tmpl_power, inverse, length):
    freq_count = spectra.shape[-1] // 2
    data_spec = spectra.astype(jnp.float32)
    tmpl_wide = tmpl_spec.astype(jnp.float32)[:, :, None, :]
    real_part = tmpl_wide[..., :freq_count] * data_spec[..., :freq_count] + tmpl_wide[..., freq_count:] * data_spec[..., freq_count:]
    imag_part = tmpl_wide[..., :freq_count] * data_spec[..., freq_count:] - tmpl_wide[..., freq_count:] * data_spec[..., :freq_count]
    product = jnp.concatenate([real_part, imag_part], axis=-1).astype(jnp.bfloat16)
    flat_rows = product.reshape(-1, product.shape[-1])
    lagged = jnp.dot(flat_rows, inverse, preferred_element_type=jnp.float32) / freq_count
    lagged = lagged.reshape(energy.shape)
    scaling = length * jnp.sqrt((energy / length + EPSILON) * (tmpl_power[..., None] + EPSILON))
    return lax.optimization_barrier(jnp.sum(lagged / scaling, axis=1))

def partial_slide(out_len):

    def slide_one(series, offset_at):
        return lax.dynamic_slice_in_dim(series, offset_at, out_len)
    return slide_one

def stack_rows(summed, shift_row, alive_mask, out_len):
    shifted = jax.vmap(partial_slide(out_len))(summed, shift_row)
    return lax.optimization_barrier(jnp.sum(jnp.where(alive_mask[:, None], shifted, 0.0), axis=0))

def reference(samples, templates, station_list, station_count, moveout, offsets):
    length = templates.shape[-1]
    forward, inverse = tables(length, 2 * length)
    blocks = station_blocks(samples, length)
    spectra = spectra_of(blocks, forward)
    energy = energy_of(blocks, length)
    tmpl_spec = spectra_of(templates, forward[:length])
    tmpl_power = lax.optimization_barrier(jnp.mean(templates.astype(jnp.float32) ** 2, axis=-1))
    shifts = moveout + offsets[station_list]
    alive_mask = lax.broadcasted_iota(jnp.int32, station_list.shape, 1) < station_count[:, None]
    out_len = energy.shape[-1] - length

    def per_template(packed):
        station_ids, spec_row, power_row, shift_row, live_row = packed
        summed = correlate(spectra[station_ids], spec_row, energy[station_ids], power_row, inverse, length)
        return stack_rows(summed, shift_row, live_row, out_len)
    stacked = lax.map(per_template, (station_list, tmpl_spec, tmpl_power, shifts, alive_mask))
    return stacked * lax.rsqrt(lax.optimization_barrier(jnp.mean(stacked * stacked, axis=-1, keepdims=True)) + EPSILON)
```

```python
import functools
import math

import jax
import jax.numpy as jnp
import numpy as np
from jax import lax
from jax.experimental import pallas as pl
from jax.experimental.pallas import tpu as pltpu
from jax.sharding import PartitionSpec as P

EPSILON = 1e-06
LANES = 128
ROWS = 8
CAPACITY = 2
MESH = pl.DeviceIdType.MESH
F32 = jnp.float32
BF16 = jnp.bfloat16


def tables(length):
    frame = 2 * length
    time = np.arange(frame)
    odd = 2 * np.arange(length) + 1
    angles = (np.outer(time, odd) % (2 * frame)).astype(np.float64) * (math.pi / frame)
    cosine, sine = np.cos(angles), np.sin(angles)
    forward = np.concatenate([cosine, -sine], axis=1)
    inverse = np.concatenate([cosine[:length].T, -sine[:length].T], axis=0)
    row = np.arange(frame)[:, None]
    col = np.arange(length)[None, :]
    band = (row >= col) & (row < col + length)
    return tuple(jnp.asarray(a.astype(np.float32), BF16) for a in (forward, inverse, band))


def iota(shape, dim):
    return lax.broadcasted_iota(jnp.int32, shape, dim)


def dot(a, b):
    return jnp.dot(a, b, preferred_element_type=F32)


def split(value):
    high = value.astype(BF16)
    return high, (value - high.astype(F32)).astype(BF16)


def third(value):
    return (value * 171) >> 9


def kernel(
    sizes,
    samples,
    templates,
    station_list,
    station_count,
    moveout,
    offsets,
    forward_hbm,
    inverse_hbm,
    band_hbm,
    out,
    forward,
    inverse,
    band,
    raw,
    traces,
    small,
    pick,
    outbox,
    inbox,
    parts,
    replies,
    answers,
    local_sem,
    part_send,
    part_recv,
    box_sem,
    back_sem,
):
    tpl, sta, stations, channels, tpl_dev, width, length = sizes
    depth = 2 * tpl
    owners = sta
    frame = 2 * length
    rows_all = owners * ROWS
    slots = CAPACITY * owners
    entries = tpl_dev * width * channels
    columns = (entries + LANES - 1) // LANES * LANES

    p = lax.axis_index("tpl")
    s = lax.axis_index("sta")
    x, z = s // depth, s % depth
    slab, half = z // 2, z % 2
    me = x * depth + 2 * p + half

    def member(o):
        return {"tpl": (o % depth) // 2, "sta": (o // depth) * depth + 2 * slab + o % 2}

    def source(i):
        return {"tpl": i, "sta": me}

    def handler(i):
        return {"tpl": slab, "sta": x * depth + 2 * i + half}

    own = jnp.where(s == me, 1, 0)

    load_raw = pltpu.make_async_copy(templates, raw, local_sem.at[0])
    load_forward = pltpu.make_async_copy(forward_hbm, forward, local_sem.at[1])
    load_band = pltpu.make_async_copy(band_hbm, band, local_sem.at[2])
    load_inverse = pltpu.make_async_copy(inverse_hbm, inverse, local_sem.at[3])
    load_raw.start()
    load_forward.start()
    load_band.start()
    load_inverse.start()

    barrier = pltpu.get_barrier_semaphore()

    def greet(i, carry):
        o = lax.rem(me + i, owners)
        pl.semaphore_signal(barrier, inc=1, device_id=member(o), device_id_type=MESH)
        return carry

    lax.fori_loop(1, owners, greet, 0)
    for i in range(tpl):

        @pl.when((s != me) | (p != i))
        def _():
            pl.semaphore_signal(barrier, inc=1, device_id=source(i), device_id_type=MESH)

    small[...] = jnp.zeros(small.shape, F32)
    stations_here = station_list[...]
    moves = moveout[...]
    small[0:tpl_dev, 0:width] = (stations_here >> 4).astype(F32)
    small[8 : 8 + tpl_dev, 0:width] = (stations_here & 15).astype(F32)
    small[16 : 16 + tpl_dev, 0:width] = (moves >> 1).astype(F32)
    small[24 : 24 + tpl_dev, 0:width] = (moves & 1).astype(F32)
    col = iota((ROWS, columns), 1)
    col_tpl = col & 3
    col_key = third(col >> 2)
    col_chan = (col >> 2) - 3 * col_key
    expand_row = iota((LANES, columns), 0)
    expand_key = third(iota((LANES, columns), 1) >> 2)
    expand = jnp.where(expand_row == expand_key, 1.0, 0.0).astype(BF16)
    spread = dot(small[...].astype(BF16), expand)
    mine = iota((ROWS, columns), 0) == col_tpl

    def flat(i):
        return jnp.sum(jnp.where(mine, spread[8 * i : 8 * i + 8], 0.0), axis=0, keepdims=True)

    owner_of, local_id, move_high, move_low = flat(0), flat(1), flat(2), flat(3)
    used = jnp.zeros((ROWS, columns), jnp.int32)
    for t in range(tpl_dev):
        used = jnp.where(col_tpl == t, station_count[t], used)
    live = (col_key < used) & (col < entries)
    owner_live = jnp.where(live[0:1], owner_of, -1.0)

    row = iota((rows_all, 1), 0)
    row_owner = (row >> 3).astype(F32)
    q = row & 7
    row_rank = jnp.where(((q >= 3) & (q < 6)) | (q == 7), 1.0, 0.0)
    row_chan = jnp.where(q >= 6, 0, jnp.where(q >= 3, q - 3, q))
    belongs = owner_live == row_owner
    up_row, up_col = iota((columns, columns), 0), iota((columns, columns), 1)
    up_chan = (up_row >> 2) - 3 * third(up_row >> 2)
    up_chan_col = (up_col >> 2) - 3 * third(up_col >> 2)
    earlier = jnp.where((up_row < up_col) & (up_chan == up_chan_col), 1.0, 0.0).astype(BF16)
    before = dot(jnp.where(belongs, 1.0, 0.0).astype(BF16), earlier)
    hot = jnp.where(
        belongs & (before == row_rank) & (col_chan[0:1] == row_chan), 1.0, 0.0
    )
    pick[...] = hot.astype(BF16)

    load_raw.wait()
    quads = raw[...].astype(F32).reshape(width * channels // 2, 2, tpl_dev, length)
    traces[...] = jnp.zeros(traces.shape, F32)
    traces[0 : width * channels // 2, 0:4, :] = quads[:, 0]
    traces[0 : width * channels // 2, 4:8, :] = quads[:, 1]
    placed = dot(pick[...], traces[...].reshape(columns, length).astype(BF16))
    ones = jnp.ones((columns, LANES), BF16)
    notes = jnp.concatenate(
        [dot((hot * v).astype(BF16), ones) for v in (local_id, move_high, move_low)], axis=1
    )
    outbox[...] = (
        jnp.where(q < 6, placed, notes).reshape(owners, ROWS, length).astype(BF16)
    )

    pl.semaphore_wait(barrier, owners - 1 + tpl - own)

    def part_copy(i):
        return pltpu.make_async_remote_copy(
            src_ref=samples,
            dst_ref=parts.at[p],
            send_sem=part_send.at[i],
            recv_sem=part_recv.at[p],
            device_id=handler(i),
            device_id_type=MESH,
        )

    for i in range(tpl):
        remote = (own == 0) | (slab != i)

        @pl.when(remote)
        def _():
            part_copy(i).start()

        @pl.when(jnp.logical_not(remote))
        def _():
            pltpu.make_async_copy(samples, parts.at[p], part_recv.at[p]).start()

    def box_copy(i):
        o = lax.rem(me + i, owners)
        return pltpu.make_async_remote_copy(
            src_ref=outbox.at[o],
            dst_ref=inbox.at[me],
            send_sem=box_sem.at[0],
            recv_sem=box_sem.at[1],
            device_id=member(o),
            device_id_type=MESH,
        )

    def post(i, carry):
        box_copy(i).start()
        return carry

    keep = pltpu.make_async_copy(outbox.at[me], inbox.at[me], box_sem.at[2])
    keep.start()
    lax.fori_loop(1, owners, post, 0)

    for i in range(tpl):
        pltpu.make_async_copy(samples, parts.at[i], part_recv.at[i]).wait()
    record = jnp.concatenate([parts[i].astype(F32) for i in range(tpl)], axis=1)
    blocks = jnp.concatenate([record[:, :frame], record[:, length : length + frame]], axis=0)
    load_forward.wait()
    spectra = dot(blocks.astype(BF16), forward[...]).astype(BF16)
    load_band.wait()
    high, low = split(blocks * blocks)
    energy = dot(high, band[...]) + dot(low, band[...])
    norm = (2.0 / (frame * length)) * lax.rsqrt(energy * (1.0 / length) + EPSILON)
    norm_high, norm_low = split(norm)
    held = stations * channels

    order_row = iota((rows_all, rows_all), 0)
    order_col = iota((rows_all, rows_all), 1)
    group, sender = order_row // owners, order_row % owners
    place = jnp.where(group < 6, (group >> 1) + 3 * (group & 1), group)
    order = jnp.where(order_col == sender * ROWS + place, 1.0, 0.0).astype(BF16)

    load_inverse.wait()
    keep.wait()
    everyone = pl.ds(0, owners - 1)
    pltpu.make_async_copy(outbox.at[everyone], inbox.at[everyone], box_sem.at[1]).wait()
    arrived = inbox[...].astype(F32).reshape(rows_all, length).astype(BF16)
    sorted_rows = dot(order, arrived)
    meta = sorted_rows[channels * slots :]
    lane = iota((slots, LANES), 1)
    ids = meta[:, 0:LANES].astype(jnp.int32)
    base = me * stations
    offset_rows = iota(offsets.shape, 0)
    offset_row = jnp.sum(
        jnp.where(offset_rows == base // LANES, offsets[...].astype(F32), 0.0),
        axis=0,
        keepdims=True,
    )
    offset_hot = jnp.where(lane == ids + base % LANES, offset_row, 0.0).astype(BF16)
    offset_of = dot(offset_hot, jnp.ones((LANES, LANES), BF16))
    shift = (
        2.0 * meta[:, LANES : 2 * LANES] + meta[:, 2 * LANES : 3 * LANES] + offset_of
    ).astype(jnp.int32)

    sums = [None] * 2
    for c in range(channels):
        trace = sorted_rows[c * slots : (c + 1) * slots]
        power = jnp.sum(trace * trace, axis=1, keepdims=True) * (1.0 / length)
        scale = lax.rsqrt(power + EPSILON)
        tspec = dot(trace.astype(BF16), forward[0:length, :]).astype(BF16).astype(F32)
        y_re, y_im = tspec[:, :length], tspec[:, length:]
        station_hot = jnp.where(
            iota((slots, stations), 1) == ids[:, :stations], 1.0, 0.0
        ).astype(BF16)
        for b in range(2):
            at = slice(b * held + c * stations, b * held + (c + 1) * stations)
            data = dot(station_hot, spectra[at])
            x_re, x_im = data[:, :length], data[:, length:]
            product = jnp.concatenate(
                [y_re * x_re + y_im * x_im, y_re * x_im - y_im * x_re], axis=1
            ).astype(BF16)
            lagged = dot(product, inverse[...])
            weight = dot(station_hot, norm_high[at]) + dot(station_hot, norm_low[at])
            term = lagged * weight * scale
            sums[b] = term if c == 0 else sums[b] + term

    tiles = [
        sums[b][:, j * LANES : (j + 1) * LANES] for b in range(2) for j in range(length // LANES)
    ]
    span = length // LANES
    for bit in (2, 1):
        chosen = (shift & (bit * LANES)) != 0
        tiles = [
            jnp.where(chosen, tiles[min(i + bit, len(tiles) - 1)], tiles[i])
            for i in range(span + bit)
        ]
    step = LANES // 2
    while step >= 1:
        chosen = (shift & step) != 0
        turned = [pltpu.roll(tile, LANES - step, 1) for tile in tiles]
        inside = lane < LANES - step
        after = turned[1:] + turned[-1:]
        tiles = [
            jnp.where(chosen, jnp.where(inside, turned[i], after[i]), tiles[i])
            for i in range(span + 1)
        ]
        step //= 2
    replies[...] = jnp.zeros(replies.shape, F32)
    for r in range(CAPACITY):
        for j in range(span):
            replies[:, r * span + j, :] = tiles[j][r * owners : (r + 1) * owners]

    def reply_copy(i):
        o = lax.rem(me + i, owners)
        return pltpu.make_async_remote_copy(
            src_ref=replies.at[o],
            dst_ref=answers.at[me],
            send_sem=back_sem.at[0],
            recv_sem=back_sem.at[1],
            device_id=member(o),
            device_id_type=MESH,
        )

    def answer(i, carry):
        reply_copy(i).start()
        return carry

    keep_back = pltpu.make_async_copy(replies.at[me], answers.at[me], back_sem.at[2])
    keep_back.start()
    lax.fori_loop(1, owners, answer, 0)

    wide = iota((4 * ROWS, columns), 0)
    wide_col = iota((4 * ROWS, columns), 1)
    of_template = jnp.where((wide & 7) == (wide_col & 3), 1.0, 0.0).astype(BF16)
    weights = lax.dot_general(
        of_template, pick[...], (((1,), (1,)), ((), ())), preferred_element_type=F32
    )
    weight_q = iota((4 * ROWS, rows_all), 1) & 7
    weight_j = iota((4 * ROWS, rows_all), 0) >> 3
    matches = (weight_q < 6) & (
        (weight_q == weight_j) | (weight_q == weight_j + 3)
    )
    weights = jnp.where(matches & (weight_j < 3), weights, 0.0).astype(BF16)

    keep_back.wait()
    pltpu.make_async_copy(replies.at[everyone], answers.at[everyone], back_sem.at[1]).wait()
    high, low = split(answers[...].reshape(rows_all, LANES))
    stacked = dot(weights, high) + dot(weights, low)
    chunks = [stacked[ROWS * j : ROWS * (j + 1)] for j in range(span)]
    square = chunks[0] * chunks[0]
    for chunk in chunks[1:]:
        square = square + chunk * chunk
    mean = jnp.sum(square, axis=1, keepdims=True) * (1.0 / length)
    root = lax.rsqrt(mean + EPSILON)
    for j in range(span):
        out[:, j * LANES : (j + 1) * LANES] = (chunks[j] * root)[:tpl_dev]

    for i in range(tpl):

        @pl.when((own == 0) | (slab != i))
        def _():
            part_copy(i).wait_send()

    pltpu.make_async_copy(outbox.at[everyone], inbox.at[everyone], box_sem.at[0]).wait()
    pltpu.make_async_copy(replies.at[everyone], answers.at[everyone], back_sem.at[0]).wait()


def on_device(samples, templates, station_list, station_count, moveout, offsets):
    stations, channels, part = samples.shape
    tpl_dev, width, _, length = templates.shape
    tpl, sta = lax.axis_size("tpl"), lax.axis_size("sta")
    sizes = (tpl, sta, stations, channels, tpl_dev, width, length)
    rows = jnp.transpose(samples, (1, 0, 2)).reshape(channels * stations, part)
    quads = jnp.transpose(templates, (1, 2, 0, 3)).reshape(width * channels, tpl_dev, length)
    offset_grid = offsets.reshape(-1, LANES)
    frame = 2 * length
    entries = tpl_dev * width * channels
    columns = (entries + LANES - 1) // LANES * LANES
    anywhere = pl.BlockSpec(memory_space=pl.ANY)
    vmem = pl.BlockSpec(memory_space=pltpu.VMEM)
    smem = pl.BlockSpec(memory_space=pltpu.SMEM)
    dma = pltpu.SemaphoreType.DMA
    return pl.pallas_call(
        functools.partial(kernel, sizes),
        out_shape=jax.ShapeDtypeStruct((tpl_dev, length), F32),
        in_specs=[anywhere, anywhere, vmem, smem, vmem, vmem, anywhere, anywhere, anywhere],
        out_specs=vmem,
        scratch_shapes=[
            pltpu.VMEM((frame, frame), BF16),
            pltpu.VMEM((frame, length), BF16),
            pltpu.VMEM((frame, length), BF16),
            pltpu.VMEM((width * channels, tpl_dev, length), BF16),
            pltpu.VMEM((columns // ROWS, ROWS, length), F32),
            pltpu.VMEM((4 * ROWS, LANES), F32),
            pltpu.VMEM((sta * ROWS, columns), BF16),
            pltpu.VMEM((sta, ROWS, length), BF16),
            pltpu.VMEM((sta, ROWS, length), BF16),
            pltpu.VMEM((tpl, channels * stations, part), BF16),
            pltpu.VMEM((sta, ROWS, LANES), F32),
            pltpu.VMEM((sta, ROWS, LANES), F32),
            dma((4,)),
            dma((tpl,)),
            dma((tpl,)),
            dma((3,)),
            dma((3,)),
        ],
        compiler_params=pltpu.CompilerParams(
            collective_id=0, has_side_effects=True, vmem_limit_bytes=48 * 2**20
        ),
        cost_estimate=pl.CostEstimate(
            flops=2 * 10**9, bytes_accessed=6 * 10**6, transcendentals=10**5
        ),
    )(rows, quads, station_list, station_count, moveout, offset_grid, *tables(length))


def solution(mesh):
    in_specs = (
        P("sta", None, "tpl"),
        P(("tpl", "sta"), None, None, None),
        P(("tpl", "sta"), None),
        P(("tpl", "sta")),
        P(("tpl", "sta"), None),
        P(),
    )
    out_specs = P(("tpl", "sta"), None)
    return jax.shard_map(
        on_device, mesh=mesh, in_specs=in_specs, out_specs=out_specs, check_vma=False
    )
```

```python
import functools
import math

import jax
import jax.numpy as jnp
import numpy as np
from jax import lax
from jax.experimental import pallas as pl
from jax.experimental.pallas import tpu as pltpu
from jax.sharding import PartitionSpec as P

EPSILON = 1e-06
LANES = 128
ROWS = 8
CAPACITY = 2
CHUNKS = 1
MESH = pl.DeviceIdType.MESH
F32 = jnp.float32
BF16 = jnp.bfloat16


def tables(length):
    frame = 2 * length
    time = np.arange(frame)
    odd = 2 * np.arange(length) + 1
    angles = (np.outer(time, odd) % (2 * frame)).astype(np.float64) * (math.pi / frame)
    cosine, sine = np.cos(angles), np.sin(angles)
    forward = np.concatenate([cosine, -sine], axis=1)
    inverse = np.concatenate([cosine[:length].T, -sine[:length].T], axis=0)
    row = np.arange(frame)[:, None]
    col = np.arange(length)[None, :]
    band = (row >= col) & (row < col + length)
    return tuple(jnp.asarray(a.astype(np.float32), BF16) for a in (forward, inverse, band))


def iota(shape, dim):
    return lax.broadcasted_iota(jnp.int32, shape, dim)


def dot(a, b):
    return jnp.dot(a, b, preferred_element_type=F32)


def split(value):
    high = value.astype(BF16)
    return high, (value - high.astype(F32)).astype(BF16)


def third(value):
    return (value * 171) >> 9


def kernel(
    sizes,
    samples,
    templates,
    list_hbm,
    count_hbm,
    moveout_hbm,
    offsets_hbm,
    forward_hbm,
    inverse_hbm,
    band_hbm,
    out,
    forward,
    inverse,
    band,
    raw,
    station_list,
    station_count,
    moveout,
    offsets,
    traces,
    small,
    pick,
    chunk_in,
    chunk_out,
    outbox,
    inbox,
    parts,
    staged,
    replies,
    answers,
    local_sem,
    part_send,
    part_recv,
    box_sem,
    back_sem,
):
    tpl, sta, stations, channels, tpl_dev, width, length, part = sizes
    depth = 2 * tpl
    owners = sta
    frame = 2 * length
    held = stations * channels
    rows_all = owners * ROWS
    slots = CAPACITY * owners
    entries = tpl_dev * width * channels
    columns = (entries + LANES - 1) // LANES * LANES
    span = length // LANES

    p = lax.axis_index("tpl")
    s = lax.axis_index("sta")
    x, z = s // depth, s % depth
    slab, half = z // 2, z % 2
    me = x * depth + 2 * p + half

    def member(i):
        o = lax.rem(me + i, owners)
        return {"tpl": (o % depth) // 2, "sta": (o // depth) * depth + 2 * slab + o % 2}

    def source(i):
        return {"tpl": i, "sta": me}

    def handler(i):
        return {"tpl": slab, "sta": x * depth + 2 * i + half}

    own = jnp.where(s == me, 1, 0)

    barrier = pltpu.get_barrier_semaphore()
    for i in range(tpl):

        @pl.when((s != me) | (p != i))
        def _():
            pl.semaphore_signal(barrier, inc=1, device_id=source(i), device_id_type=MESH)

    def greet(i, carry):
        pl.semaphore_signal(barrier, inc=1, device_id=member(i), device_id_type=MESH)
        return carry

    lax.fori_loop(1, owners, greet, 0)

    def load(n, src, dst):
        copy = pltpu.make_async_copy(src, dst, local_sem.at[n])
        copy.start()
        return copy

    load_chunk = load(8, samples, chunk_in)
    load_list = load(4, list_hbm, station_list)
    load_count = load(5, count_hbm, station_count)
    load_moveout = load(6, moveout_hbm, moveout)
    load_raw = load(0, templates, raw)
    load_offsets = load(7, offsets_hbm, offsets)
    load_forward = load(1, forward_hbm, forward)
    load_inverse = load(3, inverse_hbm, inverse)
    load_band = load(2, band_hbm, band)

    full, rest = part // LANES, part % LANES
    per = LANES // rest
    groups = held // ROWS
    load_chunk.wait()
    chunk = chunk_in[...].astype(F32)
    packed = [chunk[:, j * LANES : (j + 1) * LANES] for j in range(full)]
    for first in range(0, groups, per):
        pieces = [
            chunk[g * ROWS : (g + 1) * ROWS, full * LANES :]
            for g in range(first, min(first + per, groups))
        ]
        if len(pieces) < per:
            pieces.append(jnp.zeros((ROWS, (per - len(pieces)) * rest), F32))
        packed.append(jnp.concatenate(pieces, axis=1))
    chunk_out[...] = jnp.concatenate(packed, axis=0).astype(BF16)

    small[...] = jnp.zeros(small.shape, F32)
    load_list.wait()
    load_count.wait()
    load_moveout.wait()
    stations_here = station_list[...]
    moves = moveout[...]
    small[0:tpl_dev, 0:width] = (stations_here >> 4).astype(F32)
    small[8 : 8 + tpl_dev, 0:width] = (stations_here & 15).astype(F32)
    small[16 : 16 + tpl_dev, 0:width] = (moves >> 1).astype(F32)
    small[24 : 24 + tpl_dev, 0:width] = (moves & 1).astype(F32)
    col = iota((ROWS, columns), 1)
    col_tpl = col & 3
    col_key = third(col >> 2)
    col_chan = (col >> 2) - 3 * col_key
    expand_row = iota((LANES, columns), 0)
    expand_key = third(iota((LANES, columns), 1) >> 2)
    expand = jnp.where(expand_row == expand_key, 1.0, 0.0).astype(BF16)
    spread = dot(small[...].astype(BF16), expand)
    mine = iota((ROWS, columns), 0) == col_tpl

    def flat(i):
        return jnp.sum(jnp.where(mine, spread[8 * i : 8 * i + 8], 0.0), axis=0, keepdims=True)

    owner_of, local_id, move_high, move_low = flat(0), flat(1), flat(2), flat(3)
    used = jnp.zeros((ROWS, columns), jnp.int32)
    for t in range(tpl_dev):
        used = jnp.where(col_tpl == t, station_count[t], used)
    live = (col_key < used) & (col < entries)
    owner_live = jnp.where(live[0:1], owner_of, -1.0)

    row = iota((rows_all, 1), 0)
    row_owner = (((row >> 3) + me) & (owners - 1)).astype(F32)
    q = row & 7
    row_rank = jnp.where(((q >= 3) & (q < 6)) | (q == 7), 1.0, 0.0)
    row_chan = jnp.where(q >= 6, 0, jnp.where(q >= 3, q - 3, q))
    belongs = owner_live == row_owner
    up_row, up_col = iota((columns, columns), 0), iota((columns, columns), 1)
    up_chan = (up_row >> 2) - 3 * third(up_row >> 2)
    up_chan_col = (up_col >> 2) - 3 * third(up_col >> 2)
    earlier = jnp.where((up_row < up_col) & (up_chan == up_chan_col), 1.0, 0.0).astype(BF16)
    before = dot(jnp.where(belongs, 1.0, 0.0).astype(BF16), earlier)
    hot = jnp.where(
        belongs & (before == row_rank) & (col_chan[0:1] == row_chan), 1.0, 0.0
    )
    pick[...] = hot.astype(BF16)

    load_raw.wait()
    quads = raw[...].astype(F32).reshape(width * channels // 2, 2, tpl_dev, length)
    traces[...] = jnp.zeros(traces.shape, F32)
    traces[0 : width * channels // 2, 0:4, :] = quads[:, 0]
    traces[0 : width * channels // 2, 4:8, :] = quads[:, 1]
    placed = dot(pick[...], traces[...].reshape(columns, length).astype(BF16))
    ones = jnp.ones((columns, LANES), BF16)
    notes = jnp.concatenate(
        [dot((hot * v).astype(BF16), ones) for v in (local_id, move_high, move_low)], axis=1
    )
    outbox[...] = (
        jnp.where(q < 6, placed, notes).reshape(owners, ROWS, length).astype(BF16)
    )

    pl.semaphore_wait(barrier, owners - 1 + tpl - own)

    def part_copy(i):
        return pltpu.make_async_remote_copy(
            src_ref=chunk_out,
            dst_ref=parts.at[p],
            send_sem=part_send.at[i],
            recv_sem=part_recv.at[p],
            device_id=handler(i),
            device_id_type=MESH,
        )

    for i in range(tpl):
        remote = (own == 0) | (slab != i)

        @pl.when(remote)
        def _():
            part_copy(i).start()

        @pl.when(jnp.logical_not(remote))
        def _():
            pltpu.make_async_copy(chunk_out, parts.at[p], part_recv.at[p]).start()

    def box_copy(i):
        return pltpu.make_async_remote_copy(
            src_ref=outbox.at[i],
            dst_ref=inbox.at[owners - i],
            send_sem=box_sem.at[0],
            recv_sem=box_sem.at[1],
            device_id=member(i),
            device_id_type=MESH,
        )

    def post(i, carry):
        box_copy(i).start()
        return carry

    keep = pltpu.make_async_copy(outbox.at[0], inbox.at[0], box_sem.at[2])
    keep.start()
    lax.fori_loop(1, owners, post, 0)

    batch = owners // CHUNKS
    order_row = iota((rows_all, 1), 0)
    group, inner = order_row // slots, order_row % slots
    block, rank = inner // (CAPACITY * batch), (inner % (CAPACITY * batch)) // batch
    sender = block * batch + inner % batch
    place = jnp.where(group < channels, group + channels * rank, CAPACITY * channels + rank)
    order = jnp.where(
        iota((rows_all, rows_all), 1) == sender * ROWS + place, 1.0, 0.0
    ).astype(BF16)
    staged[...] = jnp.zeros(staged.shape, F32)
    load_offsets.wait()
    load_forward.wait()
    load_inverse.wait()
    load_band.wait()
    base = me * stations
    offset_row = jnp.sum(
        jnp.where(
            iota(offsets.shape, 0) == base // LANES, offsets[...].astype(F32), 0.0
        ),
        axis=0,
        keepdims=True,
    )

    keep.wait()
    others = pl.ds(1, owners - 1)
    pltpu.make_async_copy(outbox.at[others], inbox.at[others], box_sem.at[1]).wait()
    arrived = inbox[...].astype(F32).reshape(rows_all, length).astype(BF16)
    sorted_rows = dot(order, arrived)
    meta = sorted_rows[channels * slots :]
    lane = iota((slots, LANES), 1)
    ids = meta[:, 0:LANES].astype(jnp.int32)
    offset_hot = jnp.where(lane == ids + base % LANES, offset_row, 0.0).astype(BF16)
    offset_of = dot(offset_hot, jnp.ones((LANES, LANES), BF16))
    shift = (
        2.0 * meta[:, LANES : 2 * LANES] + meta[:, 2 * LANES : 3 * LANES] + offset_of
    ).astype(jnp.int32)
    station_hot = jnp.where(
        iota((slots, stations), 1) == ids[:, :stations], 1.0, 0.0
    ).astype(BF16)
    tracks = sorted_rows[: channels * slots]
    power = jnp.sum(tracks * tracks, axis=1, keepdims=True) * (1.0 / length)
    scale = lax.rsqrt(power + EPSILON)
    tspec = dot(tracks.astype(BF16), forward[0:length, :]).astype(BF16)

    for i in range(tpl):
        pltpu.make_async_copy(chunk_out, parts.at[i], part_recv.at[i]).wait()
    pieces = []
    for i in range(tpl):
        piece = parts[i].astype(F32)
        pieces += [piece[j * held : (j + 1) * held] for j in range(full)]
        tail = []
        for g in range(groups):
            at = full * held + g // per * ROWS
            tail.append(piece[at : at + ROWS, g % per * rest : (g % per + 1) * rest])
        pieces.append(jnp.concatenate(tail, axis=0))
    record = jnp.concatenate(pieces, axis=1)
    blocks = jnp.concatenate([record[:, :frame], record[:, length : length + frame]], axis=0)
    spectra = dot(blocks.astype(BF16), forward[...]).astype(BF16)
    high, low = split(blocks * blocks)
    energy = dot(high, band[...]) + dot(low, band[...])
    norm = (2.0 / (frame * length)) * lax.rsqrt(energy * (1.0 / length) + EPSILON)
    norm_high, norm_low = split(norm)

    def reply_copy(i):
        return pltpu.make_async_remote_copy(
            src_ref=replies.at[i],
            dst_ref=answers.at[owners - i],
            send_sem=back_sem.at[0],
            recv_sem=back_sem.at[1],
            device_id=member(i),
            device_id_type=MESH,
        )

    def answer(i, carry):
        reply_copy(i).start()
        return carry

    count = CAPACITY * batch
    for k in range(CHUNKS):
        here = slice(k * count, (k + 1) * count)
        pairs = [(c, b) for b in range(2) for c in range(channels)]
        products, weights = [], []
        for c, b in pairs:
            at = slice(b * held + c * stations, b * held + (c + 1) * stations)
            mine = slice(c * slots + k * count, c * slots + (k + 1) * count)
            y = tspec[mine].astype(F32)
            y_re, y_im = y[:, :length], y[:, length:]
            data = dot(station_hot[here], spectra[at])
            x_re, x_im = data[:, :length], data[:, length:]
            products.append(
                jnp.concatenate(
                    [y_re * x_re + y_im * x_im, y_re * x_im - y_im * x_re], axis=1
                ).astype(BF16)
            )
            weights.append(
                (dot(station_hot[here], norm_high[at]) + dot(station_hot[here], norm_low[at]))
                * scale[mine]
            )
        lagged = dot(jnp.concatenate(products, axis=0), inverse[...])
        sums = [None, None]
        for n, (c, b) in enumerate(pairs):
            term = lagged[n * count : (n + 1) * count] * weights[n]
            sums[b] = term if c == 0 else sums[b] + term
        tiles = [sums[b][:, j * LANES : (j + 1) * LANES] for b in range(2) for j in range(span)]
        turn, at_lane = shift[here], lane[here]
        for bit in (2, 1):
            chosen = (turn & (bit * LANES)) != 0
            tiles = [
                jnp.where(chosen, tiles[min(i + bit, len(tiles) - 1)], tiles[i])
                for i in range(span + bit)
            ]
        step = LANES // 2
        while step >= 1:
            chosen = (turn & step) != 0
            turned = [pltpu.roll(tile, LANES - step, 1) for tile in tiles]
            inside = at_lane < LANES - step
            after = turned[1:] + turned[-1:]
            tiles = [
                jnp.where(chosen, jnp.where(inside, turned[i], after[i]), tiles[i])
                for i in range(span + 1)
            ]
            step //= 2
        senders = slice(k * batch, (k + 1) * batch)
        for r in range(CAPACITY):
            for j in range(span):
                staged[senders, r * span + j, :] = tiles[j][r * batch : (r + 1) * batch]
        replies[senders] = staged[senders].astype(BF16)
        lax.fori_loop(max(1, k * batch), (k + 1) * batch, answer, 0)
    keep_back = pltpu.make_async_copy(replies.at[0], answers.at[0], back_sem.at[2])
    keep_back.start()

    wide = iota((4 * ROWS, columns), 0)
    wide_col = iota((4 * ROWS, columns), 1)
    of_template = jnp.where((wide & 7) == (wide_col & 3), 1.0, 0.0).astype(BF16)
    weights = lax.dot_general(
        of_template, pick[...], (((1,), (1,)), ((), ())), preferred_element_type=F32
    )
    weight_q = iota((4 * ROWS, rows_all), 1) & 7
    weight_j = iota((4 * ROWS, rows_all), 0) >> 3
    matches = (weight_q < 6) & ((weight_q == weight_j) | (weight_q == weight_j + 3))
    weights = jnp.where(matches & (weight_j < 3), weights, 0.0).astype(BF16)

    keep_back.wait()
    pltpu.make_async_copy(replies.at[others], answers.at[others], back_sem.at[1]).wait()
    stacked = dot(weights, answers[...].astype(F32).reshape(rows_all, LANES).astype(BF16))
    tops = [stacked[ROWS * j : ROWS * (j + 1)] for j in range(span)]
    square = tops[0] * tops[0]
    for top in tops[1:]:
        square = square + top * top
    mean = jnp.sum(square, axis=1, keepdims=True) * (1.0 / length)
    root = lax.rsqrt(mean + EPSILON)
    for j in range(span):
        out[:, j * LANES : (j + 1) * LANES] = (tops[j] * root)[:tpl_dev]

    for i in range(tpl):

        @pl.when((own == 0) | (slab != i))
        def _():
            part_copy(i).wait_send()

    pltpu.make_async_copy(outbox.at[others], inbox.at[others], box_sem.at[0]).wait()
    pltpu.make_async_copy(replies.at[others], answers.at[others], back_sem.at[0]).wait()


def on_device(samples, templates, station_list, station_count, moveout, offsets):
    stations, channels, part = samples.shape
    tpl_dev, width, _, length = templates.shape
    tpl, sta = lax.axis_size("tpl"), lax.axis_size("sta")
    sizes = (tpl, sta, stations, channels, tpl_dev, width, length, part)
    held = stations * channels
    packs = held // ROWS // (LANES // (part % LANES))
    packed = part // LANES * held + ROWS * max(1, packs)
    rows = jnp.transpose(samples, (1, 0, 2)).reshape(channels * stations, part)
    quads = jnp.transpose(templates, (1, 2, 0, 3)).reshape(width * channels, tpl_dev, length)
    offset_grid = offsets.reshape(-1, LANES)
    frame = 2 * length
    entries = tpl_dev * width * channels
    columns = (entries + LANES - 1) // LANES * LANES
    hbm = pl.BlockSpec(memory_space=pltpu.HBM)
    vmem = pl.BlockSpec(memory_space=pltpu.VMEM)
    dma = pltpu.SemaphoreType.DMA
    return pl.pallas_call(
        functools.partial(kernel, sizes),
        out_shape=jax.ShapeDtypeStruct((tpl_dev, length), F32),
        in_specs=[hbm] * 9,
        out_specs=vmem,
        scratch_shapes=[
            pltpu.VMEM((frame, frame), BF16),
            pltpu.VMEM((frame, length), BF16),
            pltpu.VMEM((frame, length), BF16),
            pltpu.VMEM((width * channels, tpl_dev, length), BF16),
            pltpu.VMEM(station_list.shape, jnp.int32),
            pltpu.SMEM(station_count.shape, jnp.int32),
            pltpu.VMEM(moveout.shape, jnp.int32),
            pltpu.VMEM(offset_grid.shape, jnp.int32),
            pltpu.VMEM((columns // ROWS, ROWS, length), F32),
            pltpu.VMEM((4 * ROWS, LANES), F32),
            pltpu.VMEM((sta * ROWS, columns), BF16),
            pltpu.VMEM((held, part), BF16),
            pltpu.VMEM((packed, LANES), BF16),
            pltpu.VMEM((sta, ROWS, length), BF16),
            pltpu.VMEM((sta, ROWS, length), BF16),
            pltpu.VMEM((tpl, packed, LANES), BF16),
            pltpu.VMEM((sta, ROWS, LANES), F32),
            pltpu.VMEM((sta, ROWS, LANES), BF16),
            pltpu.VMEM((sta, ROWS, LANES), BF16),
            dma((9,)),
            dma((tpl,)),
            dma((tpl,)),
            dma((3,)),
            dma((3,)),
        ],
        compiler_params=pltpu.CompilerParams(
            collective_id=0, has_side_effects=True, vmem_limit_bytes=60 * 2**20
        ),
        cost_estimate=pl.CostEstimate(
            flops=2 * 10**9, bytes_accessed=6 * 10**6, transcendentals=10**5
        ),
    )(rows, quads, station_list, station_count, moveout, offset_grid, *tables(length))


def solution(mesh):
    in_specs = (
        P("sta", None, "tpl"),
        P(("tpl", "sta"), None, None, None),
        P(("tpl", "sta"), None),
        P(("tpl", "sta")),
        P(("tpl", "sta"), None),
        P(),
    )
    out_specs = P(("tpl", "sta"), None)
    return jax.shard_map(
        on_device, mesh=mesh, in_specs=in_specs, out_specs=out_specs, check_vma=False
    )
```

```python
import functools
import math

import jax
import jax.numpy as jnp
import numpy as np
from jax import lax
from jax.experimental import pallas as pl
from jax.experimental.pallas import tpu as pltpu
from jax.sharding import PartitionSpec as P

EPSILON = 1e-06
LANES = 128
ROWS = 8
CAPACITY = 2
BOX = 16
STRIDE = 4
NEAR = (1, -1, 2, 0)
MESH = pl.DeviceIdType.MESH
F32 = jnp.float32
BF16 = jnp.bfloat16


def tables(length):
    frame = 2 * length
    time = np.arange(frame)
    odd = 2 * np.arange(length) + 1
    angles = (np.outer(time, odd) % (2 * frame)).astype(np.float64) * (math.pi / frame)
    cosine, sine = np.cos(angles), np.sin(angles)
    forward = np.concatenate([cosine, -sine], axis=1)
    inverse = np.concatenate([cosine[:length].T, -sine[:length].T], axis=0)
    row = np.arange(frame)[:, None]
    col = np.arange(length)[None, :]
    band = (row >= col) & (row < col + length)
    return tuple(jnp.asarray(a.astype(np.float32), BF16) for a in (forward, inverse, band))


def iota(shape, dim):
    return lax.broadcasted_iota(jnp.int32, shape, dim)


def dot(a, b):
    return jnp.dot(a, b, preferred_element_type=F32)


def split(value):
    high = value.astype(BF16)
    return high, (value - high.astype(F32)).astype(BF16)


def third(value):
    return (value * 171) >> 9


def kernel(
    sizes,
    samples,
    templates,
    list_hbm,
    count_hbm,
    moveout_hbm,
    offsets_hbm,
    forward_hbm,
    inverse_hbm,
    band_hbm,
    out,
    forward,
    inverse,
    band,
    raw,
    station_list,
    station_count,
    moveout,
    offsets,
    traces,
    small,
    pick,
    chunk_in,
    chunk_out,
    relay,
    outbox,
    inbox,
    parts,
    staged,
    replies,
    answers,
    local_sem,
    part_send,
    part_recv,
    relay_send,
    relay_recv,
    box_sem,
    back_sem,
):
    tpl, sta, stations, channels, tpl_dev, width, length, part = sizes
    depth = 2 * tpl
    peers = sta // 2
    relays = depth // STRIDE
    frame = 2 * length
    held = stations * channels
    pair = 2 * stations
    places = 2 * CAPACITY
    rows_all = peers * BOX
    slots = places * peers
    entries = tpl_dev * width * channels
    columns = (entries + LANES - 1) // LANES * LANES
    span = length // LANES

    p = lax.axis_index("tpl")
    s = lax.axis_index("sta")
    x, z = s // depth, s % depth
    me = x * tpl + p

    def member(i):
        d = lax.rem(me + i, peers)
        return {"tpl": d % tpl, "sta": (d // tpl) * depth + z}

    def plane(i):
        return x * depth + lax.rem(z + depth + i, depth)

    barrier = pltpu.get_barrier_semaphore()
    for k in range(1, relays):
        pl.semaphore_signal(
            barrier,
            inc=1,
            device_id={"tpl": p, "sta": plane(-STRIDE * k)},
            device_id_type=MESH,
        )
    for h in range(2):
        gap = lax.rem(z + depth - 2 * p - h, STRIDE)
        hop = jnp.where(gap == 3, -1, gap)

        @pl.when(gap != 0)
        def _():
            for i in range(tpl):
                pl.semaphore_signal(
                    barrier,
                    inc=1,
                    device_id={"tpl": i, "sta": plane(-hop)},
                    device_id_type=MESH,
                )

    def greet(i, carry):
        pl.semaphore_signal(barrier, inc=1, device_id=member(i), device_id_type=MESH)
        return carry

    lax.fori_loop(1, peers, greet, 0)

    def load(n, src, dst):
        copy = pltpu.make_async_copy(src, dst, local_sem.at[n])
        copy.start()
        return copy

    load_chunk = load(8, samples, chunk_in)
    load_list = load(4, list_hbm, station_list)
    load_count = load(5, count_hbm, station_count)
    load_moveout = load(6, moveout_hbm, moveout)
    load_raw = load(0, templates, raw)
    load_offsets = load(7, offsets_hbm, offsets)
    load_forward = load(1, forward_hbm, forward)
    load_inverse = load(3, inverse_hbm, inverse)
    load_band = load(2, band_hbm, band)

    full, rest = part // LANES, part % LANES
    per = LANES // rest
    groups = held // ROWS
    load_chunk.wait()
    chunk = chunk_in[...].astype(F32)
    packed = [chunk[:, j * LANES : (j + 1) * LANES] for j in range(full)]
    for first in range(0, groups, per):
        pieces = [
            chunk[g * ROWS : (g + 1) * ROWS, full * LANES :]
            for g in range(first, min(first + per, groups))
        ]
        if len(pieces) < per:
            pieces.append(jnp.zeros((ROWS, (per - len(pieces)) * rest), F32))
        packed.append(jnp.concatenate(pieces, axis=1))
    chunk_out[...] = jnp.concatenate(packed, axis=0).astype(BF16)

    small[...] = jnp.zeros(small.shape, F32)
    load_list.wait()
    load_count.wait()
    load_moveout.wait()
    stations_here = station_list[...]
    moves = moveout[...]
    small[0:tpl_dev, 0:width] = (stations_here >> 4).astype(F32)
    small[8 : 8 + tpl_dev, 0:width] = (stations_here & 15).astype(F32)
    small[16 : 16 + tpl_dev, 0:width] = (moves >> 1).astype(F32)
    small[24 : 24 + tpl_dev, 0:width] = (moves & 1).astype(F32)
    col = iota((ROWS, columns), 1)
    col_tpl = col & 3
    col_key = third(col >> 2)
    col_chan = (col >> 2) - 3 * col_key
    expand_row = iota((LANES, columns), 0)
    expand_key = third(iota((LANES, columns), 1) >> 2)
    expand = jnp.where(expand_row == expand_key, 1.0, 0.0).astype(BF16)
    spread = dot(small[...].astype(BF16), expand)
    mine = iota((ROWS, columns), 0) == col_tpl

    def flat(i):
        return jnp.sum(jnp.where(mine, spread[8 * i : 8 * i + 8], 0.0), axis=0, keepdims=True)

    owner_of, local_id, move_high, move_low = flat(0), flat(1), flat(2), flat(3)
    used = jnp.zeros((ROWS, columns), jnp.int32)
    for t in range(tpl_dev):
        used = jnp.where(col_tpl == t, station_count[t], used)
    live = (col_key < used) & (col < entries)
    owner_live = jnp.where(live[0:1], owner_of, -1.0)

    row = iota((rows_all, 1), 0)
    q = row & (BOX - 1)
    traced = q < channels * places
    row_place = jnp.where(traced, third(q), q - channels * places)
    row_chan = jnp.where(traced, q - channels * row_place, 0)
    row_rank = (row_place & 1).astype(F32)
    row_peer = ((row >> 4) + me) & (peers - 1)
    row_owner = (2 * row_peer + (row_place >> 1)).astype(F32)
    belongs = owner_live == row_owner
    up_row, up_col = iota((columns, columns), 0), iota((columns, columns), 1)
    up_chan = (up_row >> 2) - 3 * third(up_row >> 2)
    up_chan_col = (up_col >> 2) - 3 * third(up_col >> 2)
    earlier = jnp.where((up_row < up_col) & (up_chan == up_chan_col), 1.0, 0.0).astype(BF16)
    before = dot(jnp.where(belongs, 1.0, 0.0).astype(BF16), earlier)
    hot = jnp.where(
        belongs & (before == row_rank) & (col_chan[0:1] == row_chan), 1.0, 0.0
    )
    pick[...] = hot.astype(BF16)

    load_raw.wait()
    quads = raw[...].astype(F32).reshape(width * channels // 2, 2, tpl_dev, length)
    traces[...] = jnp.zeros(traces.shape, F32)
    traces[0 : width * channels // 2, 0:4, :] = quads[:, 0]
    traces[0 : width * channels // 2, 4:8, :] = quads[:, 1]
    placed = dot(pick[...], traces[...].reshape(columns, length).astype(BF16))
    ones = jnp.ones((columns, LANES), BF16)
    notes = jnp.concatenate(
        [dot((hot * v).astype(BF16), ones) for v in (local_id, move_high, move_low)], axis=1
    )
    outbox[...] = (
        jnp.where(traced, placed, notes).reshape(peers, BOX, length).astype(BF16)
    )

    pl.semaphore_wait(barrier, peers - 1 + relays - 1 + relays * (len(NEAR) - 1))

    def relay_copy(k):
        return pltpu.make_async_remote_copy(
            src_ref=chunk_out,
            dst_ref=relay.at[k],
            send_sem=relay_send.at[k],
            recv_sem=relay_recv.at[k],
            device_id={"tpl": p, "sta": plane(STRIDE * k)},
            device_id_type=MESH,
        )

    def part_copy(k, n):
        origin = lax.rem(z + depth - STRIDE * k, depth)
        return pltpu.make_async_remote_copy(
            src_ref=relay.at[k] if k else chunk_out,
            dst_ref=parts.at[(origin % 2) * tpl + p],
            send_sem=part_send.at[k * len(NEAR) + n],
            recv_sem=part_recv.at[(origin % 2) * tpl + p],
            device_id={"tpl": origin // 2, "sta": plane(NEAR[n])},
            device_id_type=MESH,
        )

    def stays(k):
        return lax.rem(z + depth - STRIDE * k, depth) // 2 == p

    def spread_part(k):
        for n in range(len(NEAR)):
            if NEAR[n]:
                part_copy(k, n).start()
                continue

            @pl.when(jnp.logical_not(stays(k)))
            def _():
                part_copy(k, n).start()

            @pl.when(stays(k))
            def _():
                origin = lax.rem(z + depth - STRIDE * k, depth)
                place = (origin % 2) * tpl + p
                pltpu.make_async_copy(
                    relay.at[k] if k else chunk_out, parts.at[place], part_recv.at[place]
                ).start()

    for k in range(1, relays):
        relay_copy(k).start()
    spread_part(0)

    def box_copy(i):
        return pltpu.make_async_remote_copy(
            src_ref=outbox.at[i],
            dst_ref=inbox.at[peers - i],
            send_sem=box_sem.at[0],
            recv_sem=box_sem.at[1],
            device_id=member(i),
            device_id_type=MESH,
        )

    def post(i, carry):
        box_copy(i).start()
        return carry

    keep = pltpu.make_async_copy(outbox.at[0], inbox.at[0], box_sem.at[2])
    keep.start()
    lax.fori_loop(1, peers, post, 0)
    for k in range(1, relays):
        relay_copy(k).wait_recv()
        spread_part(k)

    order_row = iota((rows_all, 1), 0)
    group, inner = order_row // slots, order_row % slots
    place, sender = inner // peers, inner % peers
    at_row = jnp.where(group < channels, group + channels * place, channels * places + place)
    order = jnp.where(
        iota((rows_all, rows_all), 1) == sender * BOX + at_row, 1.0, 0.0
    ).astype(BF16)
    staged[...] = jnp.zeros(staged.shape, F32)
    load_offsets.wait()
    load_forward.wait()
    load_inverse.wait()
    load_band.wait()
    base = me * pair
    offset_row = jnp.sum(
        jnp.where(
            iota(offsets.shape, 0) == base // LANES, offsets[...].astype(F32), 0.0
        ),
        axis=0,
        keepdims=True,
    )

    keep.wait()
    others = pl.ds(1, peers - 1)
    pltpu.make_async_copy(outbox.at[others], inbox.at[others], box_sem.at[1]).wait()
    arrived = inbox[...].astype(F32).reshape(rows_all, length).astype(BF16)
    sorted_rows = dot(order, arrived)
    meta = sorted_rows[channels * slots :]
    lane = iota((slots, LANES), 1)
    block = iota((slots, LANES), 0) // (CAPACITY * peers)
    ids = meta[:, 0:LANES].astype(jnp.int32) + stations * block
    offset_hot = jnp.where(lane == ids + base % LANES, offset_row, 0.0).astype(BF16)
    offset_of = dot(offset_hot, jnp.ones((LANES, LANES), BF16))
    shift = (
        2.0 * meta[:, LANES : 2 * LANES] + meta[:, 2 * LANES : 3 * LANES] + offset_of
    ).astype(jnp.int32)
    station_hot = jnp.where(
        iota((slots, pair), 1) == ids[:, :pair], 1.0, 0.0
    ).astype(BF16)
    tracks = sorted_rows[: channels * slots]
    power = jnp.sum(tracks * tracks, axis=1, keepdims=True) * (1.0 / length)
    scale = lax.rsqrt(power + EPSILON)
    tspec = dot(tracks.astype(BF16), forward[0:length, :]).astype(BF16)

    for i in range(2 * tpl):
        pltpu.make_async_copy(chunk_out, parts.at[i], part_recv.at[i]).wait()
    records = []
    for h in range(2):
        pieces = []
        for i in range(tpl):
            piece = parts[h * tpl + i].astype(F32)
            pieces += [piece[j * held : (j + 1) * held] for j in range(full)]
            tail = []
            for g in range(groups):
                at = full * held + g // per * ROWS
                tail.append(piece[at : at + ROWS, g % per * rest : (g % per + 1) * rest])
            pieces.append(jnp.concatenate(tail, axis=0))
        records.append(jnp.concatenate(pieces, axis=1))
    blocks = jnp.concatenate(
        [
            records[h][c * stations : (c + 1) * stations, b * length : b * length + frame]
            for b in range(2)
            for c in range(channels)
            for h in range(2)
        ],
        axis=0,
    )
    spectra = dot(blocks.astype(BF16), forward[...]).astype(BF16)
    high, low = split(blocks * blocks)
    energy = dot(high, band[...]) + dot(low, band[...])
    norm = (2.0 / (frame * length)) * lax.rsqrt(energy * (1.0 / length) + EPSILON)
    norm_high, norm_low = split(norm)

    def reply_copy(i):
        return pltpu.make_async_remote_copy(
            src_ref=replies.at[i],
            dst_ref=answers.at[peers - i],
            send_sem=back_sem.at[0],
            recv_sem=back_sem.at[1],
            device_id=member(i),
            device_id_type=MESH,
        )

    def answer(i, carry):
        reply_copy(i).start()
        return carry

    pairs = [(c, b) for b in range(2) for c in range(channels)]
    products, weights = [], []
    for c, b in pairs:
        at = slice((b * channels + c) * pair, (b * channels + c + 1) * pair)
        mine = slice(c * slots, (c + 1) * slots)
        y = tspec[mine].astype(F32)
        y_re, y_im = y[:, :length], y[:, length:]
        data = dot(station_hot, spectra[at])
        x_re, x_im = data[:, :length], data[:, length:]
        products.append(
            jnp.concatenate(
                [y_re * x_re + y_im * x_im, y_re * x_im - y_im * x_re], axis=1
            ).astype(BF16)
        )
        weights.append(
            (dot(station_hot, norm_high[at]) + dot(station_hot, norm_low[at])) * scale[mine]
        )
    lagged = dot(jnp.concatenate(products, axis=0), inverse[...])
    sums = [None, None]
    for n, (c, b) in enumerate(pairs):
        term = lagged[n * slots : (n + 1) * slots] * weights[n]
        sums[b] = term if c == 0 else sums[b] + term
    tiles = [sums[b][:, j * LANES : (j + 1) * LANES] for b in range(2) for j in range(span)]
    for bit in (2, 1):
        chosen = (shift & (bit * LANES)) != 0
        tiles = [
            jnp.where(chosen, tiles[min(i + bit, len(tiles) - 1)], tiles[i])
            for i in range(span + bit)
        ]
    step = LANES // 2
    while step >= 1:
        chosen = (shift & step) != 0
        turned = [pltpu.roll(tile, LANES - step, 1) for tile in tiles]
        inside = lane < LANES - step
        after = turned[1:] + turned[-1:]
        tiles = [
            jnp.where(chosen, jnp.where(inside, turned[i], after[i]), tiles[i])
            for i in range(span + 1)
        ]
        step //= 2
    for i in range(places):
        for j in range(span):
            staged[:, i * span + j, :] = tiles[j][i * peers : (i + 1) * peers]
    replies[...] = staged[...].astype(BF16)
    lax.fori_loop(1, peers, answer, 0)
    keep_back = pltpu.make_async_copy(replies.at[0], answers.at[0], back_sem.at[2])
    keep_back.start()

    wide = iota((4 * ROWS, columns), 0)
    wide_col = iota((4 * ROWS, columns), 1)
    of_template = jnp.where((wide & 7) == (wide_col & 3), 1.0, 0.0).astype(BF16)
    weights = lax.dot_general(
        of_template, pick[...], (((1,), (1,)), ((), ())), preferred_element_type=F32
    )
    weight_q = iota((4 * ROWS, rows_all), 1) & (BOX - 1)
    weight_j = iota((4 * ROWS, rows_all), 0) >> 3
    matches = (weight_q < span * places) & (weight_q - span * third(weight_q) == weight_j)
    weights = jnp.where(matches, weights, 0.0).astype(BF16)

    keep_back.wait()
    pltpu.make_async_copy(replies.at[others], answers.at[others], back_sem.at[1]).wait()
    stacked = dot(weights, answers[...].astype(F32).reshape(rows_all, LANES).astype(BF16))
    tops = [stacked[ROWS * j : ROWS * (j + 1)] for j in range(span)]
    square = tops[0] * tops[0]
    for top in tops[1:]:
        square = square + top * top
    mean = jnp.sum(square, axis=1, keepdims=True) * (1.0 / length)
    root = lax.rsqrt(mean + EPSILON)
    for j in range(span):
        out[:, j * LANES : (j + 1) * LANES] = (tops[j] * root)[:tpl_dev]

    for k in range(relays):
        if k:
            relay_copy(k).wait_send()
        for n in range(len(NEAR)):
            if NEAR[n]:
                part_copy(k, n).wait_send()
                continue

            @pl.when(jnp.logical_not(stays(k)))
            def _():
                part_copy(k, n).wait_send()

    pltpu.make_async_copy(outbox.at[others], inbox.at[others], box_sem.at[0]).wait()
    pltpu.make_async_copy(replies.at[others], answers.at[others], back_sem.at[0]).wait()


def on_device(samples, templates, station_list, station_count, moveout, offsets):
    stations, channels, part = samples.shape
    tpl_dev, width, _, length = templates.shape
    tpl, sta = lax.axis_size("tpl"), lax.axis_size("sta")
    sizes = (tpl, sta, stations, channels, tpl_dev, width, length, part)
    held = stations * channels
    packs = -(-(held // ROWS) // (LANES // (part % LANES)))
    packed = part // LANES * held + ROWS * packs
    rows = jnp.transpose(samples, (1, 0, 2)).reshape(channels * stations, part)
    quads = jnp.transpose(templates, (1, 2, 0, 3)).reshape(width * channels, tpl_dev, length)
    offset_grid = offsets.reshape(-1, LANES)
    frame = 2 * length
    entries = tpl_dev * width * channels
    columns = (entries + LANES - 1) // LANES * LANES
    hbm = pl.BlockSpec(memory_space=pltpu.HBM)
    vmem = pl.BlockSpec(memory_space=pltpu.VMEM)
    dma = pltpu.SemaphoreType.DMA
    return pl.pallas_call(
        functools.partial(kernel, sizes),
        out_shape=jax.ShapeDtypeStruct((tpl_dev, length), F32),
        in_specs=[hbm] * 9,
        out_specs=vmem,
        scratch_shapes=[
            pltpu.VMEM((frame, frame), BF16),
            pltpu.VMEM((frame, length), BF16),
            pltpu.VMEM((frame, length), BF16),
            pltpu.VMEM((width * channels, tpl_dev, length), BF16),
            pltpu.VMEM(station_list.shape, jnp.int32),
            pltpu.SMEM(station_count.shape, jnp.int32),
            pltpu.VMEM(moveout.shape, jnp.int32),
            pltpu.VMEM(offset_grid.shape, jnp.int32),
            pltpu.VMEM((columns // ROWS, ROWS, length), F32),
            pltpu.VMEM((4 * ROWS, LANES), F32),
            pltpu.VMEM((sta * ROWS, columns), BF16),
            pltpu.VMEM((held, part), BF16),
            pltpu.VMEM((packed, LANES), BF16),
            pltpu.VMEM((2 * tpl // STRIDE, packed, LANES), BF16),
            pltpu.VMEM((sta // 2, BOX, length), BF16),
            pltpu.VMEM((sta // 2, BOX, length), BF16),
            pltpu.VMEM((2 * tpl, packed, LANES), BF16),
            pltpu.VMEM((sta // 2, BOX, LANES), F32),
            pltpu.VMEM((sta // 2, BOX, LANES), BF16),
            pltpu.VMEM((sta // 2, BOX, LANES), BF16),
            dma((9,)),
            dma((8 * tpl // STRIDE,)),
            dma((2 * tpl,)),
            dma((2 * tpl // STRIDE,)),
            dma((2 * tpl // STRIDE,)),
            dma((3,)),
            dma((3,)),
        ],
        compiler_params=pltpu.CompilerParams(
            collective_id=0, has_side_effects=True, vmem_limit_bytes=60 * 2**20
        ),
        cost_estimate=pl.CostEstimate(
            flops=2 * 10**9, bytes_accessed=6 * 10**6, transcendentals=10**5
        ),
    )(rows, quads, station_list, station_count, moveout, offset_grid, *tables(length))


def solution(mesh):
    in_specs = (
        P("sta", None, "tpl"),
        P(("tpl", "sta"), None, None, None),
        P(("tpl", "sta"), None),
        P(("tpl", "sta")),
        P(("tpl", "sta"), None),
        P(),
    )
    out_specs = P(("tpl", "sta"), None)
    return jax.shard_map(
        on_device, mesh=mesh, in_specs=in_specs, out_specs=out_specs, check_vma=False
    )
```

```python
import functools
import math

import jax
import jax.numpy as jnp
import numpy as np
from jax import lax
from jax.experimental import pallas as pl
from jax.experimental.pallas import tpu as pltpu
from jax.sharding import PartitionSpec as P

EPSILON = 1e-06
LANES = 128
ROWS = 8
CAPACITY = 2
BOX = 16
STRIDE = 4
SHIFT = 2
TURN = 13
NEAR = (1, -1, 2, 0)
MESH = pl.DeviceIdType.MESH
F32 = jnp.float32
BF16 = jnp.bfloat16


def tables(length):
    frame = 2 * length
    time = np.arange(frame)
    odd = 2 * np.arange(length) + 1
    angles = (np.outer(time, odd) % (2 * frame)).astype(np.float64) * (math.pi / frame)
    cosine, sine = np.cos(angles), np.sin(angles)
    forward = np.concatenate([cosine, -sine], axis=1)
    inverse = np.concatenate([cosine[:length].T, -sine[:length].T], axis=0)
    row = np.arange(frame)[:, None]
    col = np.arange(length)[None, :]
    band = (row >= col) & (row < col + length)
    return tuple(jnp.asarray(a.astype(np.float32), BF16) for a in (forward, inverse, band))


def iota(shape, dim):
    return lax.broadcasted_iota(jnp.int32, shape, dim)


def dot(a, b):
    return jnp.dot(a, b, preferred_element_type=F32)


def split(value):
    high = value.astype(BF16)
    return high, (value - high.astype(F32)).astype(BF16)


def third(value):
    return (value * 171) >> 9


def kernel(
    sizes,
    samples,
    templates,
    list_hbm,
    count_hbm,
    moveout_hbm,
    offsets_hbm,
    forward_hbm,
    inverse_hbm,
    band_hbm,
    out,
    forward,
    inverse,
    band,
    raw,
    station_list,
    station_count,
    moveout,
    offsets,
    traces,
    small,
    pick,
    chunk_in,
    chunk_out,
    relay,
    outbox,
    inbox,
    parts,
    staged,
    replies,
    answers,
    local_sem,
    part_send,
    part_recv,
    relay_send,
    relay_recv,
    box_sem,
    back_sem,
):
    tpl, sta, stations, channels, tpl_dev, width, length, part = sizes
    depth = 2 * tpl
    peers = sta // 2
    relays = depth // STRIDE
    frame = 2 * length
    held = stations * channels
    pair = 2 * stations
    places = 2 * CAPACITY
    rows_all = peers * BOX
    slots = places * peers
    entries = tpl_dev * width * channels
    columns = (entries + LANES - 1) // LANES * LANES
    span = length // LANES

    p = lax.axis_index("tpl")
    s = lax.axis_index("sta")
    x, z = s // depth, s % depth
    me = x * tpl + p

    def member(i):
        d = lax.rem(me + i, peers)
        return {"tpl": d % tpl, "sta": (d // tpl) * depth + z}

    def far(k):
        return STRIDE * k + SHIFT

    def plane(i):
        return x * depth + lax.rem(z + 2 * depth + i, depth)

    def load(n, src, dst):
        copy = pltpu.make_async_copy(src, dst, local_sem.at[n])
        copy.start()
        return copy

    load_chunk = load(8, samples, chunk_in)

    barrier = pltpu.get_barrier_semaphore()
    for k in range(relays):
        pl.semaphore_signal(
            barrier,
            inc=1,
            device_id={"tpl": p, "sta": plane(-far(k))},
            device_id_type=MESH,
        )
    for h in range(2):
        gap = lax.rem(z + 2 * depth - SHIFT - 2 * p - h, STRIDE)
        hop = jnp.where(gap == 3, -1, gap)

        @pl.when(gap != 0)
        def _():
            for i in range(tpl):
                pl.semaphore_signal(
                    barrier,
                    inc=1,
                    device_id={"tpl": i, "sta": plane(-hop)},
                    device_id_type=MESH,
                )

    def greet(i, carry):
        pl.semaphore_signal(barrier, inc=1, device_id=member(i), device_id_type=MESH)
        return carry

    lax.fori_loop(1, peers, greet, 0)

    load_list = load(4, list_hbm, station_list)
    load_count = load(5, count_hbm, station_count)
    load_moveout = load(6, moveout_hbm, moveout)
    load_raw = load(0, templates, raw)
    load_offsets = load(7, offsets_hbm, offsets)
    load_forward = load(1, forward_hbm, forward)
    load_inverse = load(3, inverse_hbm, inverse)
    load_band = load(2, band_hbm, band)

    full, rest = part // LANES, part % LANES
    per = LANES // rest
    groups = held // ROWS
    load_chunk.wait()
    chunk = chunk_in[...].astype(F32)
    packed = [chunk[:, j * LANES : (j + 1) * LANES] for j in range(full)]
    for first in range(0, groups, per):
        pieces = [
            chunk[g * ROWS : (g + 1) * ROWS, full * LANES :]
            for g in range(first, min(first + per, groups))
        ]
        if len(pieces) < per:
            pieces.append(jnp.zeros((ROWS, (per - len(pieces)) * rest), F32))
        packed.append(jnp.concatenate(pieces, axis=1))
    chunk_out[...] = jnp.concatenate(packed, axis=0).astype(BF16)

    pl.semaphore_wait(barrier, peers - 1 + relays + relays * (len(NEAR) - 1))

    def relay_copy(k):
        return pltpu.make_async_remote_copy(
            src_ref=chunk_out,
            dst_ref=relay.at[k],
            send_sem=relay_send.at[k],
            recv_sem=relay_recv.at[k],
            device_id={"tpl": p, "sta": plane(far(k))},
            device_id_type=MESH,
        )

    def part_copy(k, n):
        origin = lax.rem(z + 2 * depth - far(k), depth)
        return pltpu.make_async_remote_copy(
            src_ref=relay.at[k],
            dst_ref=parts.at[(origin % 2) * tpl + p],
            send_sem=part_send.at[k * len(NEAR) + n],
            recv_sem=part_recv.at[(origin % 2) * tpl + p],
            device_id={"tpl": origin // 2, "sta": plane(NEAR[n])},
            device_id_type=MESH,
        )

    def stays(k):
        return lax.rem(z + 2 * depth - far(k), depth) // 2 == p

    def spread_part(k):
        for n in range(len(NEAR)):
            if NEAR[n]:
                part_copy(k, n).start()
                continue

            @pl.when(jnp.logical_not(stays(k)))
            def _():
                part_copy(k, n).start()

            @pl.when(stays(k))
            def _():
                origin = lax.rem(z + 2 * depth - far(k), depth)
                place = (origin % 2) * tpl + p
                pltpu.make_async_copy(
                    relay.at[k], parts.at[place], part_recv.at[place]
                ).start()

    for k in sorted(range(relays), key=lambda k: -min(far(k), depth - far(k))):
        relay_copy(k).start()

    small[...] = jnp.zeros(small.shape, F32)
    load_list.wait()
    load_count.wait()
    load_moveout.wait()
    stations_here = station_list[...]
    moves = moveout[...]
    small[0:tpl_dev, 0:width] = (stations_here >> 4).astype(F32)
    small[8 : 8 + tpl_dev, 0:width] = (stations_here & 15).astype(F32)
    small[16 : 16 + tpl_dev, 0:width] = (moves >> 1).astype(F32)
    small[24 : 24 + tpl_dev, 0:width] = (moves & 1).astype(F32)
    col = iota((ROWS, columns), 1)
    col_tpl = col & 3
    col_key = third(col >> 2)
    col_chan = (col >> 2) - 3 * col_key
    expand_row = iota((LANES, columns), 0)
    expand_key = third(iota((LANES, columns), 1) >> 2)
    expand = jnp.where(expand_row == expand_key, 1.0, 0.0).astype(BF16)
    spread = dot(small[...].astype(BF16), expand)
    mine = iota((ROWS, columns), 0) == col_tpl

    def flat(i):
        return jnp.sum(jnp.where(mine, spread[8 * i : 8 * i + 8], 0.0), axis=0, keepdims=True)

    owner_of, local_id, move_high, move_low = flat(0), flat(1), flat(2), flat(3)
    used = jnp.zeros((ROWS, columns), jnp.int32)
    for t in range(tpl_dev):
        used = jnp.where(col_tpl == t, station_count[t], used)
    live = (col_key < used) & (col < entries)
    owner_live = jnp.where(live[0:1], owner_of, -1.0)

    row = iota((rows_all, 1), 0)
    q = row & (BOX - 1)
    traced = q < channels * places
    row_place = jnp.where(traced, third(q), q - channels * places)
    row_chan = jnp.where(traced, q - channels * row_place, 0)
    row_rank = (row_place & 1).astype(F32)
    row_peer = ((row >> 4) + me) & (peers - 1)
    row_owner = (2 * row_peer + (row_place >> 1)).astype(F32)
    belongs = owner_live == row_owner
    up_row, up_col = iota((columns, columns), 0), iota((columns, columns), 1)
    up_chan = (up_row >> 2) - 3 * third(up_row >> 2)
    up_chan_col = (up_col >> 2) - 3 * third(up_col >> 2)
    earlier = jnp.where((up_row < up_col) & (up_chan == up_chan_col), 1.0, 0.0).astype(BF16)
    before = dot(jnp.where(belongs, 1.0, 0.0).astype(BF16), earlier)
    hot = jnp.where(
        belongs & (before == row_rank) & (col_chan[0:1] == row_chan), 1.0, 0.0
    )
    pick[...] = hot.astype(BF16)

    load_raw.wait()
    quads = raw[...].astype(F32).reshape(width * channels // 2, 2, tpl_dev, length)
    traces[...] = jnp.zeros(traces.shape, F32)
    traces[0 : width * channels // 2, 0:4, :] = quads[:, 0]
    traces[0 : width * channels // 2, 4:8, :] = quads[:, 1]
    placed = dot(pick[...], traces[...].reshape(columns, length).astype(BF16))
    ones = jnp.ones((columns, LANES), BF16)
    notes = jnp.concatenate(
        [dot((hot * v).astype(BF16), ones) for v in (local_id, move_high, move_low)], axis=1
    )
    outbox[...] = (
        jnp.where(traced, placed, notes).reshape(peers, BOX, length).astype(BF16)
    )

    def box_copy(i):
        return pltpu.make_async_remote_copy(
            src_ref=outbox.at[i],
            dst_ref=inbox.at[peers - i],
            send_sem=box_sem.at[0],
            recv_sem=box_sem.at[1],
            device_id=member(i),
            device_id_type=MESH,
        )

    def post(i, carry):
        box_copy(lax.rem(i * TURN, peers)).start()
        return carry

    keep = pltpu.make_async_copy(outbox.at[0], inbox.at[0], box_sem.at[2])
    keep.start()
    lax.fori_loop(1, peers, post, 0)
    for k in sorted(range(relays), key=lambda k: min(far(k), depth - far(k))):
        relay_copy(k).wait_recv()
        spread_part(k)

    order_row = iota((rows_all, 1), 0)
    group, inner = order_row // slots, order_row % slots
    place, sender = inner // peers, inner % peers
    at_row = jnp.where(group < channels, group + channels * place, channels * places + place)
    order = jnp.where(
        iota((rows_all, rows_all), 1) == sender * BOX + at_row, 1.0, 0.0
    ).astype(BF16)
    staged[...] = jnp.zeros(staged.shape, F32)
    load_offsets.wait()
    load_forward.wait()
    load_inverse.wait()
    load_band.wait()
    base = me * pair
    offset_row = jnp.sum(
        jnp.where(
            iota(offsets.shape, 0) == base // LANES, offsets[...].astype(F32), 0.0
        ),
        axis=0,
        keepdims=True,
    )

    keep.wait()
    others = pl.ds(1, peers - 1)
    pltpu.make_async_copy(outbox.at[others], inbox.at[others], box_sem.at[1]).wait()
    arrived = inbox[...].astype(F32).reshape(rows_all, length).astype(BF16)
    sorted_rows = dot(order, arrived)
    meta = sorted_rows[channels * slots :]
    lane = iota((slots, LANES), 1)
    block = iota((slots, LANES), 0) // (CAPACITY * peers)
    ids = meta[:, 0:LANES].astype(jnp.int32) + stations * block
    offset_hot = jnp.where(lane == ids + base % LANES, offset_row, 0.0).astype(BF16)
    offset_of = dot(offset_hot, jnp.ones((LANES, LANES), BF16))
    shift = (
        2.0 * meta[:, LANES : 2 * LANES] + meta[:, 2 * LANES : 3 * LANES] + offset_of
    ).astype(jnp.int32)
    station_hot = jnp.where(
        iota((slots, pair), 1) == ids[:, :pair], 1.0, 0.0
    ).astype(BF16)
    tracks = sorted_rows[: channels * slots]
    power = jnp.sum(tracks * tracks, axis=1, keepdims=True) * (1.0 / length)
    scale = lax.rsqrt(power + EPSILON)
    tspec = dot(tracks.astype(BF16), forward[0:length, :]).astype(BF16)

    wide = iota((4 * ROWS, columns), 0)
    wide_col = iota((4 * ROWS, columns), 1)
    of_template = jnp.where((wide & 7) == (wide_col & 3), 1.0, 0.0).astype(BF16)
    of_rows = lax.dot_general(
        of_template, pick[...], (((1,), (1,)), ((), ())), preferred_element_type=F32
    )
    weight_q = iota((4 * ROWS, rows_all), 1) & (BOX - 1)
    weight_j = iota((4 * ROWS, rows_all), 0) >> 3
    matches = (weight_q < span * places) & (weight_q - span * third(weight_q) == weight_j)
    of_rows = jnp.where(matches, of_rows, 0.0).astype(BF16)

    for i in range(2 * tpl):
        pltpu.make_async_copy(chunk_out, parts.at[i], part_recv.at[i]).wait()
    records = []
    for h in range(2):
        pieces = []
        for i in range(tpl):
            piece = parts[h * tpl + i].astype(F32)
            pieces += [piece[j * held : (j + 1) * held] for j in range(full)]
            tail = []
            for g in range(groups):
                at = full * held + g // per * ROWS
                tail.append(piece[at : at + ROWS, g % per * rest : (g % per + 1) * rest])
            pieces.append(jnp.concatenate(tail, axis=0))
        records.append(jnp.concatenate(pieces, axis=1))
    blocks = jnp.concatenate(
        [
            records[h][c * stations : (c + 1) * stations, b * length : b * length + frame]
            for b in range(2)
            for c in range(channels)
            for h in range(2)
        ],
        axis=0,
    )
    spectra = dot(blocks.astype(BF16), forward[...]).astype(BF16)
    high, low = split(blocks * blocks)
    energy = dot(high, band[...]) + dot(low, band[...])
    norm = (2.0 / (frame * length)) * lax.rsqrt(energy * (1.0 / length) + EPSILON)
    norm_high, norm_low = split(norm)

    def reply_copy(i):
        return pltpu.make_async_remote_copy(
            src_ref=replies.at[i],
            dst_ref=answers.at[peers - i],
            send_sem=back_sem.at[0],
            recv_sem=back_sem.at[1],
            device_id=member(i),
            device_id_type=MESH,
        )

    def answer(i, carry):
        reply_copy(lax.rem(i * TURN, peers)).start()
        return carry

    pairs = [(c, b) for b in range(2) for c in range(channels)]
    products, weights = [], []
    for c, b in pairs:
        at = slice((b * channels + c) * pair, (b * channels + c + 1) * pair)
        mine = slice(c * slots, (c + 1) * slots)
        y = tspec[mine].astype(F32)
        y_re, y_im = y[:, :length], y[:, length:]
        data = dot(station_hot, spectra[at])
        x_re, x_im = data[:, :length], data[:, length:]
        products.append(
            jnp.concatenate(
                [y_re * x_re + y_im * x_im, y_re * x_im - y_im * x_re], axis=1
            ).astype(BF16)
        )
        weights.append(
            (dot(station_hot, norm_high[at]) + dot(station_hot, norm_low[at])) * scale[mine]
        )
    lagged = dot(jnp.concatenate(products, axis=0), inverse[...])
    sums = [None, None]
    for n, (c, b) in enumerate(pairs):
        term = lagged[n * slots : (n + 1) * slots] * weights[n]
        sums[b] = term if c == 0 else sums[b] + term
    tiles = [sums[b][:, j * LANES : (j + 1) * LANES] for b in range(2) for j in range(span)]
    for bit in (2, 1):
        chosen = (shift & (bit * LANES)) != 0
        tiles = [
            jnp.where(chosen, tiles[min(i + bit, len(tiles) - 1)], tiles[i])
            for i in range(span + bit)
        ]
    step = LANES // 2
    while step >= 1:
        chosen = (shift & step) != 0
        turned = [pltpu.roll(tile, LANES - step, 1) for tile in tiles]
        inside = lane < LANES - step
        after = turned[1:] + turned[-1:]
        tiles = [
            jnp.where(chosen, jnp.where(inside, turned[i], after[i]), tiles[i])
            for i in range(span + 1)
        ]
        step //= 2
    for i in range(places):
        for j in range(span):
            staged[:, i * span + j, :] = tiles[j][i * peers : (i + 1) * peers]
    replies[...] = staged[...].astype(BF16)
    lax.fori_loop(1, peers, answer, 0)
    keep_back = pltpu.make_async_copy(replies.at[0], answers.at[0], back_sem.at[2])
    keep_back.start()

    keep_back.wait()
    pltpu.make_async_copy(replies.at[others], answers.at[others], back_sem.at[1]).wait()
    stacked = dot(of_rows, answers[...].astype(F32).reshape(rows_all, LANES).astype(BF16))
    tops = [stacked[ROWS * j : ROWS * (j + 1)] for j in range(span)]
    square = tops[0] * tops[0]
    for top in tops[1:]:
        square = square + top * top
    mean = jnp.sum(square, axis=1, keepdims=True) * (1.0 / length)
    root = lax.rsqrt(mean + EPSILON)
    for j in range(span):
        out[:, j * LANES : (j + 1) * LANES] = (tops[j] * root)[:tpl_dev]

    for k in range(relays):
        relay_copy(k).wait_send()
        for n in range(len(NEAR)):
            if NEAR[n]:
                part_copy(k, n).wait_send()
                continue

            @pl.when(jnp.logical_not(stays(k)))
            def _():
                part_copy(k, n).wait_send()

    pltpu.make_async_copy(outbox.at[others], inbox.at[others], box_sem.at[0]).wait()
    pltpu.make_async_copy(replies.at[others], answers.at[others], back_sem.at[0]).wait()


def on_device(samples, templates, station_list, station_count, moveout, offsets):
    stations, channels, part = samples.shape
    tpl_dev, width, _, length = templates.shape
    tpl, sta = lax.axis_size("tpl"), lax.axis_size("sta")
    sizes = (tpl, sta, stations, channels, tpl_dev, width, length, part)
    held = stations * channels
    packs = -(-(held // ROWS) // (LANES // (part % LANES)))
    packed = part // LANES * held + ROWS * packs
    rows = jnp.transpose(samples, (1, 0, 2)).reshape(channels * stations, part)
    quads = jnp.transpose(templates, (1, 2, 0, 3)).reshape(width * channels, tpl_dev, length)
    offset_grid = offsets.reshape(-1, LANES)
    frame = 2 * length
    entries = tpl_dev * width * channels
    columns = (entries + LANES - 1) // LANES * LANES
    hbm = pl.BlockSpec(memory_space=pltpu.HBM)
    vmem = pl.BlockSpec(memory_space=pltpu.VMEM)
    dma = pltpu.SemaphoreType.DMA
    return pl.pallas_call(
        functools.partial(kernel, sizes),
        out_shape=jax.ShapeDtypeStruct((tpl_dev, length), F32),
        in_specs=[hbm] * 9,
        out_specs=vmem,
        scratch_shapes=[
            pltpu.VMEM((frame, frame), BF16),
            pltpu.VMEM((frame, length), BF16),
            pltpu.VMEM((frame, length), BF16),
            pltpu.VMEM((width * channels, tpl_dev, length), BF16),
            pltpu.VMEM(station_list.shape, jnp.int32),
            pltpu.SMEM(station_count.shape, jnp.int32),
            pltpu.VMEM(moveout.shape, jnp.int32),
            pltpu.VMEM(offset_grid.shape, jnp.int32),
            pltpu.VMEM((columns // ROWS, ROWS, length), F32),
            pltpu.VMEM((4 * ROWS, LANES), F32),
            pltpu.VMEM((sta * ROWS, columns), BF16),
            pltpu.VMEM((held, part), BF16),
            pltpu.VMEM((packed, LANES), BF16),
            pltpu.VMEM((2 * tpl // STRIDE, packed, LANES), BF16),
            pltpu.VMEM((sta // 2, BOX, length), BF16),
            pltpu.VMEM((sta // 2, BOX, length), BF16),
            pltpu.VMEM((2 * tpl, packed, LANES), BF16),
            pltpu.VMEM((sta // 2, BOX, LANES), F32),
            pltpu.VMEM((sta // 2, BOX, LANES), BF16),
            pltpu.VMEM((sta // 2, BOX, LANES), BF16),
            dma((9,)),
            dma((8 * tpl // STRIDE,)),
            dma((2 * tpl,)),
            dma((2 * tpl // STRIDE,)),
            dma((2 * tpl // STRIDE,)),
            dma((3,)),
            dma((3,)),
        ],
        compiler_params=pltpu.CompilerParams(
            collective_id=0, has_side_effects=True, vmem_limit_bytes=60 * 2**20
        ),
        cost_estimate=pl.CostEstimate(
            flops=2 * 10**9, bytes_accessed=6 * 10**6, transcendentals=10**5
        ),
    )(rows, quads, station_list, station_count, moveout, offset_grid, *tables(length))


def solution(mesh):
    in_specs = (
        P("sta", None, "tpl"),
        P(("tpl", "sta"), None, None, None),
        P(("tpl", "sta"), None),
        P(("tpl", "sta")),
        P(("tpl", "sta"), None),
        P(),
    )
    out_specs = P(("tpl", "sta"), None)
    return jax.shard_map(
        on_device, mesh=mesh, in_specs=in_specs, out_specs=out_specs, check_vma=False
    )
```

```python
import functools
import math

import jax
import jax.numpy as jnp
import numpy as np
from jax import lax
from jax.experimental import pallas as pl
from jax.experimental.pallas import tpu as pltpu
from jax.sharding import PartitionSpec as P

EPSILON = 1e-06
LANES = 128
ROWS = 8
CAPACITY = 2
BOX = 16
TURN = 13
ROUTES = (
    (4, (4, 3, 2, 1, 0, -1)),
    (-4, (-3, -2, -1, 0, 1)),
    (0, (2, -2, 1, -1, 0)),
)
MESH = pl.DeviceIdType.MESH
F32 = jnp.float32
BF16 = jnp.bfloat16


def tables(length):
    frame = 2 * length
    time = np.arange(frame)
    odd = 2 * np.arange(length) + 1
    angles = (np.outer(time, odd) % (2 * frame)).astype(np.float64) * (math.pi / frame)
    cosine, sine = np.cos(angles), np.sin(angles)
    forward = np.concatenate([cosine, -sine], axis=1)
    inverse = np.concatenate([cosine[:length].T, -sine[:length].T], axis=0)
    row = np.arange(frame)[:, None]
    col = np.arange(length)[None, :]
    band = (row >= col) & (row < col + length)
    return tuple(jnp.asarray(a.astype(np.float32), BF16) for a in (forward, inverse, band))


def iota(shape, dim):
    return lax.broadcasted_iota(jnp.int32, shape, dim)


def dot(a, b):
    return jnp.dot(a, b, preferred_element_type=F32)


def third(value):
    return (value * 171) >> 9


def kernel(
    sizes,
    samples,
    templates,
    list_hbm,
    count_hbm,
    moveout_hbm,
    offsets_hbm,
    forward_hbm,
    inverse_hbm,
    band_hbm,
    out,
    forward,
    inverse,
    band,
    raw,
    station_list,
    station_count,
    moveout,
    offsets,
    traces,
    small,
    pick,
    chunk_in,
    chunk_out,
    relay,
    outbox,
    inbox,
    parts,
    staged,
    replies,
    answers,
    local_sem,
    part_send,
    part_recv,
    relay_send,
    relay_recv,
    box_sem,
    back_sem,
):
    tpl, sta, stations, channels, tpl_dev, width, length, part = sizes
    depth = 2 * tpl
    peers = sta // 2
    hops = [(k, n) for k, (far, near) in enumerate(ROUTES) for n in near]
    relays = [k for k, (far, near) in enumerate(ROUTES) if far]
    frame = 2 * length
    held = stations * channels
    pair = 2 * stations
    places = 2 * CAPACITY
    rows_all = peers * BOX
    slots = places * peers
    entries = tpl_dev * width * channels
    columns = (entries + LANES - 1) // LANES * LANES
    span = length // LANES

    p = lax.axis_index("tpl")
    s = lax.axis_index("sta")
    x, z = s // depth, s % depth
    me = x * tpl + p

    def turn(j):
        return lax.rem((j + 1) * TURN, peers)

    def member(i):
        d = lax.rem(me + i, peers)
        return {"tpl": d % tpl, "sta": (d // tpl) * depth + z}

    def plane(i):
        return x * depth + lax.rem(z + 2 * depth + i, depth)

    def load(n, src, dst):
        copy = pltpu.make_async_copy(src, dst, local_sem.at[n])
        copy.start()
        return copy

    load_chunk = load(8, samples, chunk_in)

    barrier = pltpu.get_barrier_semaphore()
    for k in relays:
        pl.semaphore_signal(
            barrier,
            inc=1,
            device_id={"tpl": p, "sta": plane(-ROUTES[k][0])},
            device_id_type=MESH,
        )
    for h in range(2):
        gap = lax.rem(z + depth - 2 * p - h, depth)
        hop = 0
        for k, n in hops:
            hop = jnp.where(gap == (ROUTES[k][0] + n) % depth, n, hop)

        @pl.when(hop != 0)
        def _():
            for i in range(tpl):
                pl.semaphore_signal(
                    barrier,
                    inc=1,
                    device_id={"tpl": i, "sta": plane(-hop)},
                    device_id_type=MESH,
                )

    def greet(i, carry):
        pl.semaphore_signal(
            barrier, inc=1, device_id=member(turn(i)), device_id_type=MESH
        )
        return carry

    lax.fori_loop(0, peers - 1, greet, 0)

    load_list = load(4, list_hbm, station_list)
    load_count = load(5, count_hbm, station_count)
    load_moveout = load(6, moveout_hbm, moveout)
    load_raw = load(0, templates, raw)
    load_offsets = load(7, offsets_hbm, offsets)
    load_forward = load(1, forward_hbm, forward)
    load_inverse = load(3, inverse_hbm, inverse)
    load_band = load(2, band_hbm, band)

    full, rest = part // LANES, part % LANES
    per = LANES // rest
    groups = held // ROWS
    load_chunk.wait()
    chunk = chunk_in[...].astype(F32)
    packed = [chunk[:, j * LANES : (j + 1) * LANES] for j in range(full)]
    for first in range(0, groups, per):
        pieces = [
            chunk[g * ROWS : (g + 1) * ROWS, full * LANES :]
            for g in range(first, min(first + per, groups))
        ]
        if len(pieces) < per:
            pieces.append(jnp.zeros((ROWS, (per - len(pieces)) * rest), F32))
        packed.append(jnp.concatenate(pieces, axis=1))
    chunk_out[...] = jnp.concatenate(packed, axis=0).astype(BF16)

    pl.semaphore_wait(barrier, peers - 1 + len(relays) + sum(n != 0 for k, n in hops))

    def relay_copy(k):
        return pltpu.make_async_remote_copy(
            src_ref=chunk_out,
            dst_ref=relay.at[k],
            send_sem=relay_send.at[k],
            recv_sem=relay_recv.at[k],
            device_id={"tpl": p, "sta": plane(ROUTES[k][0])},
            device_id_type=MESH,
        )

    def part_copy(k, n):
        origin = lax.rem(z + 2 * depth - ROUTES[k][0], depth)
        return pltpu.make_async_remote_copy(
            src_ref=relay.at[k] if ROUTES[k][0] else chunk_out,
            dst_ref=parts.at[(origin % 2) * tpl + p],
            send_sem=part_send.at[hops.index((k, n))],
            recv_sem=part_recv.at[(origin % 2) * tpl + p],
            device_id={"tpl": origin // 2, "sta": plane(n)},
            device_id_type=MESH,
        )

    def stays(k):
        return lax.rem(z + 2 * depth - ROUTES[k][0], depth) // 2 == p

    def spread_part(k):
        for n in ROUTES[k][1]:
            if n:
                part_copy(k, n).start()
                continue

            @pl.when(jnp.logical_not(stays(k)))
            def _():
                part_copy(k, n).start()

            @pl.when(stays(k))
            def _():
                origin = lax.rem(z + 2 * depth - ROUTES[k][0], depth)
                place = (origin % 2) * tpl + p
                pltpu.make_async_copy(
                    relay.at[k] if ROUTES[k][0] else chunk_out, parts.at[place], part_recv.at[place]
                ).start()

    for k in relays:
        relay_copy(k).start()
    for k in range(len(ROUTES)):
        if k not in relays:
            spread_part(k)

    small[...] = jnp.zeros(small.shape, F32)
    load_list.wait()
    load_count.wait()
    load_moveout.wait()
    stations_here = station_list[...]
    moves = moveout[...]
    small[0:tpl_dev, 0:width] = (stations_here >> 4).astype(F32)
    small[8 : 8 + tpl_dev, 0:width] = (stations_here & 15).astype(F32)
    small[16 : 16 + tpl_dev, 0:width] = (moves >> 1).astype(F32)
    small[24 : 24 + tpl_dev, 0:width] = (moves & 1).astype(F32)
    col = iota((ROWS, columns), 1)
    col_tpl = col & 3
    col_key = third(col >> 2)
    col_chan = (col >> 2) - 3 * col_key
    expand_row = iota((LANES, columns), 0)
    expand_key = third(iota((LANES, columns), 1) >> 2)
    expand = jnp.where(expand_row == expand_key, 1.0, 0.0).astype(BF16)
    spread = dot(small[...].astype(BF16), expand)
    mine = iota((ROWS, columns), 0) == col_tpl

    def flat(i):
        return jnp.sum(jnp.where(mine, spread[8 * i : 8 * i + 8], 0.0), axis=0, keepdims=True)

    owner_of, local_id, move_high, move_low = flat(0), flat(1), flat(2), flat(3)
    used = jnp.zeros((ROWS, columns), jnp.int32)
    for t in range(tpl_dev):
        used = jnp.where(col_tpl == t, station_count[t], used)
    live = (col_key < used) & (col < entries)
    owner_live = jnp.where(live[0:1], owner_of, -1.0)

    row = iota((rows_all, 1), 0)
    q = row & (BOX - 1)
    traced = q < channels * places
    row_place = jnp.where(traced, third(q), q - channels * places)
    row_chan = jnp.where(traced, q - channels * row_place, 0)
    row_rank = (row_place & 1).astype(F32)
    row_peer = ((row >> 4) + me) & (peers - 1)
    row_owner = (2 * row_peer + (row_place >> 1)).astype(F32)
    belongs = owner_live == row_owner
    up_row, up_col = iota((columns, columns), 0), iota((columns, columns), 1)
    up_chan = (up_row >> 2) - 3 * third(up_row >> 2)
    up_chan_col = (up_col >> 2) - 3 * third(up_col >> 2)
    earlier = jnp.where((up_row < up_col) & (up_chan == up_chan_col), 1.0, 0.0).astype(BF16)
    before = dot(jnp.where(belongs, 1.0, 0.0).astype(BF16), earlier)
    hot = jnp.where(
        belongs & (before == row_rank) & (col_chan[0:1] == row_chan), 1.0, 0.0
    )
    pick[...] = hot.astype(BF16)

    load_raw.wait()
    quads = raw[...].astype(F32).reshape(width * channels // 2, 2, tpl_dev, length)
    traces[...] = jnp.zeros(traces.shape, F32)
    traces[0 : width * channels // 2, 0:4, :] = quads[:, 0]
    traces[0 : width * channels // 2, 4:8, :] = quads[:, 1]
    placed = dot(pick[...], traces[...].reshape(columns, length).astype(BF16))
    ones = jnp.ones((columns, LANES), BF16)
    notes = jnp.concatenate(
        [dot((hot * v).astype(BF16), ones) for v in (local_id, move_high, move_low)], axis=1
    )
    outbox[...] = (
        jnp.where(traced, placed, notes).reshape(peers, BOX, length).astype(BF16)
    )

    def box_copy(i):
        return pltpu.make_async_remote_copy(
            src_ref=outbox.at[i],
            dst_ref=inbox.at[peers - i],
            send_sem=box_sem.at[0],
            recv_sem=box_sem.at[1],
            device_id=member(i),
            device_id_type=MESH,
        )

    def post(i, carry):
        box_copy(turn(i)).start()
        return carry

    keep = pltpu.make_async_copy(outbox.at[0], inbox.at[0], box_sem.at[2])
    keep.start()
    lax.fori_loop(0, peers - 1, post, 0)
    for k in relays:
        relay_copy(k).wait_recv()
        spread_part(k)

    order_row = iota((rows_all, 1), 0)
    group, inner = order_row // slots, order_row % slots
    place, sender = inner // peers, inner % peers
    at_row = jnp.where(group < channels, group + channels * place, channels * places + place)
    order = jnp.where(
        iota((rows_all, rows_all), 1) == sender * BOX + at_row, 1.0, 0.0
    ).astype(BF16)
    staged[...] = jnp.zeros(staged.shape, F32)
    load_offsets.wait()
    load_forward.wait()
    load_inverse.wait()
    load_band.wait()
    base = me * pair
    offset_row = jnp.sum(
        jnp.where(
            iota(offsets.shape, 0) == base // LANES, offsets[...].astype(F32), 0.0
        ),
        axis=0,
        keepdims=True,
    )

    keep.wait()
    others = pl.ds(1, peers - 1)
    pltpu.make_async_copy(outbox.at[others], inbox.at[others], box_sem.at[1]).wait()
    arrived = inbox[...].astype(F32).reshape(rows_all, length).astype(BF16)
    sorted_rows = dot(order, arrived)
    meta = sorted_rows[channels * slots :]
    lane = iota((slots, LANES), 1)
    block = iota((slots, LANES), 0) // (CAPACITY * peers)
    ids = meta[:, 0:LANES].astype(jnp.int32) + stations * block
    offset_hot = jnp.where(lane == ids + base % LANES, offset_row, 0.0).astype(BF16)
    offset_of = dot(offset_hot, jnp.ones((LANES, LANES), BF16))
    shift = (
        2.0 * meta[:, LANES : 2 * LANES] + meta[:, 2 * LANES : 3 * LANES] + offset_of
    ).astype(jnp.int32)
    station_hot = jnp.where(
        iota((slots, pair), 1) == ids[:, :pair], 1.0, 0.0
    ).astype(BF16)
    tracks = sorted_rows[: channels * slots]
    power = jnp.sum(tracks * tracks, axis=1, keepdims=True) * (1.0 / length)
    scale = lax.rsqrt(power + EPSILON)
    tspec = dot(tracks.astype(BF16), forward[0:length, :]) * scale

    wide = iota((4 * ROWS, columns), 0)
    wide_col = iota((4 * ROWS, columns), 1)
    of_template = jnp.where((wide & 7) == (wide_col & 3), 1.0, 0.0).astype(BF16)
    of_rows = lax.dot_general(
        of_template, pick[...], (((1,), (1,)), ((), ())), preferred_element_type=F32
    )
    weight_q = iota((4 * ROWS, rows_all), 1) & (BOX - 1)
    weight_j = iota((4 * ROWS, rows_all), 0) >> 3
    matches = (weight_q < span * places) & (weight_q - span * third(weight_q) == weight_j)
    of_rows = jnp.where(matches, of_rows, 0.0).astype(BF16)

    for i in range(2 * tpl):
        pltpu.make_async_copy(chunk_out, parts.at[i], part_recv.at[i]).wait()
    records = []
    for h in range(2):
        pieces = []
        for i in range(tpl):
            piece = parts[h * tpl + i].astype(F32)
            pieces += [piece[j * held : (j + 1) * held] for j in range(full)]
            tail = []
            for g in range(groups):
                at = full * held + g // per * ROWS
                tail.append(piece[at : at + ROWS, g % per * rest : (g % per + 1) * rest])
            pieces.append(jnp.concatenate(tail, axis=0))
        records.append(jnp.concatenate(pieces, axis=1))
    blocks = jnp.concatenate(
        [
            records[h][c * stations : (c + 1) * stations, b * length : b * length + frame]
            for b in range(2)
            for c in range(channels)
            for h in range(2)
        ],
        axis=0,
    )
    spectra = dot(blocks.astype(BF16), forward[...]).astype(BF16)
    energy = dot((blocks * blocks).astype(BF16), band[...])
    norm = (2.0 / (frame * length)) * lax.rsqrt(energy * (1.0 / length) + EPSILON)
    norm = norm.astype(BF16)

    def reply_copy(i):
        return pltpu.make_async_remote_copy(
            src_ref=replies.at[i],
            dst_ref=answers.at[peers - i],
            send_sem=back_sem.at[0],
            recv_sem=back_sem.at[1],
            device_id=member(i),
            device_id_type=MESH,
        )

    def answer(i, carry):
        reply_copy(turn(i)).start()
        return carry

    pairs = [(c, b) for b in range(2) for c in range(channels)]
    products, weights = [], []
    for c, b in pairs:
        at = slice((b * channels + c) * pair, (b * channels + c + 1) * pair)
        mine = slice(c * slots, (c + 1) * slots)
        y = tspec[mine]
        y_re, y_im = y[:, :length], y[:, length:]
        data = dot(station_hot, spectra[at])
        x_re, x_im = data[:, :length], data[:, length:]
        products.append(
            jnp.concatenate(
                [y_re * x_re + y_im * x_im, y_re * x_im - y_im * x_re], axis=1
            ).astype(BF16)
        )
        weights.append(dot(station_hot, norm[at]))
    lagged = dot(jnp.concatenate(products, axis=0), inverse[...])
    sums = [None, None]
    for n, (c, b) in enumerate(pairs):
        term = lagged[n * slots : (n + 1) * slots] * weights[n]
        sums[b] = term if c == 0 else sums[b] + term
    tiles = [sums[b][:, j * LANES : (j + 1) * LANES] for b in range(2) for j in range(span)]
    for bit in (2, 1):
        chosen = (shift & (bit * LANES)) != 0
        tiles = [
            jnp.where(chosen, tiles[min(i + bit, len(tiles) - 1)], tiles[i])
            for i in range(span + bit)
        ]
    step = LANES // 2
    while step >= 1:
        chosen = (shift & step) != 0
        turned = [pltpu.roll(tile, LANES - step, 1) for tile in tiles]
        inside = lane < LANES - step
        after = turned[1:] + turned[-1:]
        tiles = [
            jnp.where(chosen, jnp.where(inside, turned[i], after[i]), tiles[i])
            for i in range(span + 1)
        ]
        step //= 2
    for i in range(places):
        for j in range(span):
            staged[:, i * span + j, :] = tiles[j][i * peers : (i + 1) * peers]
    replies[...] = staged[...].astype(BF16)
    lax.fori_loop(0, peers - 1, answer, 0)
    keep_back = pltpu.make_async_copy(replies.at[0], answers.at[0], back_sem.at[2])
    keep_back.start()

    keep_back.wait()
    pltpu.make_async_copy(replies.at[others], answers.at[others], back_sem.at[1]).wait()
    stacked = dot(of_rows, answers[...].astype(F32).reshape(rows_all, LANES).astype(BF16))
    tops = [stacked[ROWS * j : ROWS * (j + 1)] for j in range(span)]
    square = tops[0] * tops[0]
    for top in tops[1:]:
        square = square + top * top
    mean = jnp.sum(square, axis=1, keepdims=True) * (1.0 / length)
    root = lax.rsqrt(mean + EPSILON)
    for j in range(span):
        out[:, j * LANES : (j + 1) * LANES] = tops[j] * root

    for k in range(len(ROUTES)):
        if k in relays:
            relay_copy(k).wait_send()
        for n in ROUTES[k][1]:
            if n:
                part_copy(k, n).wait_send()
                continue

            @pl.when(jnp.logical_not(stays(k)))
            def _():
                part_copy(k, n).wait_send()

    pltpu.make_async_copy(outbox.at[others], inbox.at[others], box_sem.at[0]).wait()
    pltpu.make_async_copy(replies.at[others], answers.at[others], back_sem.at[0]).wait()


def on_device(samples, templates, station_list, station_count, moveout, offsets):
    stations, channels, part = samples.shape
    tpl_dev, width, _, length = templates.shape
    tpl, sta = lax.axis_size("tpl"), lax.axis_size("sta")
    sizes = (tpl, sta, stations, channels, tpl_dev, width, length, part)
    held = stations * channels
    packs = -(-(held // ROWS) // (LANES // (part % LANES)))
    packed = part // LANES * held + ROWS * packs
    rows = jnp.transpose(samples, (1, 0, 2)).reshape(channels * stations, part)
    quads = jnp.transpose(templates, (1, 2, 0, 3)).reshape(width * channels, tpl_dev, length)
    offset_grid = offsets.reshape(-1, LANES)
    frame = 2 * length
    entries = tpl_dev * width * channels
    columns = (entries + LANES - 1) // LANES * LANES
    hbm = pl.BlockSpec(memory_space=pltpu.HBM)
    vmem = pl.BlockSpec(memory_space=pltpu.VMEM)
    dma = pltpu.SemaphoreType.DMA
    scaled = pl.pallas_call(
        functools.partial(kernel, sizes),
        out_shape=jax.ShapeDtypeStruct((ROWS, length), F32),
        in_specs=[hbm] * 9,
        out_specs=vmem,
        scratch_shapes=[
            pltpu.VMEM((frame, frame), BF16),
            pltpu.VMEM((frame, length), BF16),
            pltpu.VMEM((frame, length), BF16),
            pltpu.VMEM((width * channels, tpl_dev, length), BF16),
            pltpu.VMEM(station_list.shape, jnp.int32),
            pltpu.SMEM(station_count.shape, jnp.int32),
            pltpu.VMEM(moveout.shape, jnp.int32),
            pltpu.VMEM(offset_grid.shape, jnp.int32),
            pltpu.VMEM((columns // ROWS, ROWS, length), F32),
            pltpu.VMEM((4 * ROWS, LANES), F32),
            pltpu.VMEM((sta * ROWS, columns), BF16),
            pltpu.VMEM((held, part), BF16),
            pltpu.VMEM((packed, LANES), BF16),
            pltpu.VMEM((len(ROUTES), packed, LANES), BF16),
            pltpu.VMEM((sta // 2, BOX, length), BF16),
            pltpu.VMEM((sta // 2, BOX, length), BF16),
            pltpu.VMEM((2 * tpl, packed, LANES), BF16),
            pltpu.VMEM((sta // 2, BOX, LANES), F32),
            pltpu.VMEM((sta // 2, BOX, LANES), BF16),
            pltpu.VMEM((sta // 2, BOX, LANES), BF16),
            dma((9,)),
            dma((2 * tpl,)),
            dma((2 * tpl,)),
            dma((len(ROUTES),)),
            dma((len(ROUTES),)),
            dma((3,)),
            dma((3,)),
        ],
        compiler_params=pltpu.CompilerParams(
            collective_id=0, has_side_effects=True, vmem_limit_bytes=60 * 2**20
        ),
        cost_estimate=pl.CostEstimate(
            flops=2 * 10**9, bytes_accessed=6 * 10**6, transcendentals=10**5
        ),
    )(rows, quads, station_list, station_count, moveout, offset_grid, *tables(length))
    return scaled[:tpl_dev]


def solution(mesh):
    in_specs = (
        P("sta", None, "tpl"),
        P(("tpl", "sta"), None, None, None),
        P(("tpl", "sta"), None),
        P(("tpl", "sta")),
        P(("tpl", "sta"), None),
        P(),
    )
    out_specs = P(("tpl", "sta"), None)
    return jax.shard_map(
        on_device, mesh=mesh, in_specs=in_specs, out_specs=out_specs, check_vma=False
    )
```

```python
import functools
import math

import jax
import jax.numpy as jnp
import numpy as np
from jax import lax
from jax.experimental import pallas as pl
from jax.experimental.pallas import tpu as pltpu
from jax.sharding import PartitionSpec as P

EPSILON = 1e-06
LANES = 128
ROWS = 8
CAPACITY = 2
BOX = 16
TURN = 13
ROUTES = ((5, (3, 2, 1, 0, -1, -2)), (-5, (-2, -1, 0, 1, 2)), (0, (2, -2, 1, -1, 0)))
MESH = pl.DeviceIdType.MESH
F32 = jnp.float32
BF16 = jnp.bfloat16


def tables(length):
    frame = 2 * length
    time = np.arange(frame)
    odd = 2 * np.arange(length) + 1
    angles = (np.outer(time, odd) % (2 * frame)).astype(np.float64) * (math.pi / frame)
    cosine, sine = np.cos(angles), np.sin(angles)
    forward = np.concatenate([cosine, -sine], axis=1)
    inverse = np.concatenate([cosine[:length].T, -sine[:length].T], axis=0)
    row = np.arange(frame)[:, None]
    col = np.arange(length)[None, :]
    band = (row >= col) & (row < col + length)
    return tuple(jnp.asarray(a.astype(np.float32), BF16) for a in (forward, inverse, band))


def iota(shape, dim):
    return lax.broadcasted_iota(jnp.int32, shape, dim)


def dot(a, b):
    return jnp.dot(a, b, preferred_element_type=F32)


def third(value):
    return (value * 171) >> 9


def kernel(
    sizes,
    samples,
    templates,
    list_hbm,
    count_hbm,
    moveout_hbm,
    offsets_hbm,
    forward_hbm,
    inverse_hbm,
    band_hbm,
    out,
    forward,
    inverse,
    band,
    raw,
    station_list,
    station_count,
    moveout,
    offsets,
    traces,
    small,
    pick,
    chunk_in,
    chunk_out,
    relay,
    outbox,
    inbox,
    parts,
    staged,
    replies,
    answers,
    local_sem,
    part_send,
    part_recv,
    relay_send,
    relay_recv,
    box_sem,
    back_sem,
):
    tpl, sta, stations, channels, tpl_dev, width, length, part = sizes
    depth = 2 * tpl
    peers = sta // 2
    hops = [(k, n) for k, (far, near) in enumerate(ROUTES) for n in near]
    relays = [k for k, (far, near) in enumerate(ROUTES) if far]
    frame = 2 * length
    held = stations * channels
    pair = 2 * stations
    places = 2 * CAPACITY
    rows_all = peers * BOX
    slots = places * peers
    entries = tpl_dev * width * channels
    columns = (entries + LANES - 1) // LANES * LANES
    span = length // LANES

    p = lax.axis_index("tpl")
    s = lax.axis_index("sta")
    x, z = lax.div(s, depth), lax.rem(s, depth)
    me = x * tpl + p

    def turn(j):
        return (j + 1) * TURN % peers

    def member(i):
        d = lax.rem(me + i, peers)
        return {"tpl": lax.rem(d, tpl), "sta": lax.div(d, tpl) * depth + z}

    def plane(i):
        return x * depth + lax.rem(z + 2 * depth + i, depth)

    def load(n, src, dst):
        copy = pltpu.make_async_copy(src, dst, local_sem.at[n])
        copy.start()
        return copy

    load_chunk = load(8, samples, chunk_in)

    barrier = pltpu.get_barrier_semaphore()
    for k in relays:
        pl.semaphore_signal(
            barrier,
            inc=1,
            device_id={"tpl": p, "sta": plane(-ROUTES[k][0])},
            device_id_type=MESH,
        )
    for h in range(2):
        gap = lax.rem(z + depth - 2 * p - h, depth)
        hop = 0
        for k, n in hops:
            hop = jnp.where(gap == (ROUTES[k][0] + n) % depth, n, hop)

        @pl.when(hop != 0)
        def _():
            for i in range(tpl):
                pl.semaphore_signal(
                    barrier,
                    inc=1,
                    device_id={"tpl": i, "sta": plane(-hop)},
                    device_id_type=MESH,
                )

    def greet(i, carry):
        pl.semaphore_signal(
            barrier, inc=1, device_id=member(turn(i)), device_id_type=MESH
        )
        return carry

    for j in range(peers - 1):
        greet(j, 0)

    load_list = load(4, list_hbm, station_list)
    load_count = load(5, count_hbm, station_count)
    load_moveout = load(6, moveout_hbm, moveout)
    load_raw = load(0, templates, raw)
    load_offsets = load(7, offsets_hbm, offsets)
    load_forward = load(1, forward_hbm, forward)
    load_inverse = load(3, inverse_hbm, inverse)
    load_band = load(2, band_hbm, band)

    full, rest = part // LANES, part % LANES
    per = LANES // rest
    groups = held // ROWS
    load_chunk.wait()
    chunk = chunk_in[...].astype(F32)
    packed = [chunk[:, j * LANES : (j + 1) * LANES] for j in range(full)]
    for first in range(0, groups, per):
        pieces = [
            chunk[g * ROWS : (g + 1) * ROWS, full * LANES :]
            for g in range(first, min(first + per, groups))
        ]
        if len(pieces) < per:
            pieces.append(jnp.zeros((ROWS, (per - len(pieces)) * rest), F32))
        packed.append(jnp.concatenate(pieces, axis=1))
    chunk_out[...] = jnp.concatenate(packed, axis=0).astype(BF16)

    pl.semaphore_wait(barrier, peers - 1 + len(relays) + sum(n != 0 for k, n in hops))

    def relay_copy(k):
        return pltpu.make_async_remote_copy(
            src_ref=chunk_out,
            dst_ref=relay.at[k],
            send_sem=relay_send.at[k],
            recv_sem=relay_recv.at[k],
            device_id={"tpl": p, "sta": plane(ROUTES[k][0])},
            device_id_type=MESH,
        )

    def part_copy(k, n):
        origin = lax.rem(z + 2 * depth - ROUTES[k][0], depth)
        return pltpu.make_async_remote_copy(
            src_ref=relay.at[k] if ROUTES[k][0] else chunk_out,
            dst_ref=parts.at[lax.rem(origin, 2) * tpl + p],
            send_sem=part_send.at[hops.index((k, n))],
            recv_sem=part_recv.at[lax.rem(origin, 2) * tpl + p],
            device_id={"tpl": lax.div(origin, 2), "sta": plane(n)},
            device_id_type=MESH,
        )

    def stays(k):
        return lax.rem(z + 2 * depth - ROUTES[k][0], depth) // 2 == p

    def spread_part(k):
        for n in ROUTES[k][1]:
            if n:
                part_copy(k, n).start()
                continue

            @pl.when(jnp.logical_not(stays(k)))
            def _():
                part_copy(k, n).start()

            @pl.when(stays(k))
            def _():
                origin = lax.rem(z + 2 * depth - ROUTES[k][0], depth)
                place = lax.rem(origin, 2) * tpl + p
                pltpu.make_async_copy(
                    relay.at[k] if ROUTES[k][0] else chunk_out, parts.at[place], part_recv.at[place]
                ).start()

    for k in relays:
        relay_copy(k).start()
    for k in range(len(ROUTES)):
        if k not in relays:
            spread_part(k)

    small[...] = jnp.zeros(small.shape, F32)
    load_list.wait()
    load_count.wait()
    load_moveout.wait()
    stations_here = station_list[...]
    moves = moveout[...]
    small[0:tpl_dev, 0:width] = (stations_here >> 4).astype(F32)
    small[8 : 8 + tpl_dev, 0:width] = (stations_here & 15).astype(F32)
    small[16 : 16 + tpl_dev, 0:width] = (moves >> 1).astype(F32)
    small[24 : 24 + tpl_dev, 0:width] = (moves & 1).astype(F32)
    col = iota((ROWS, columns), 1)
    col_tpl = col & 3
    col_key = third(col >> 2)
    col_chan = (col >> 2) - 3 * col_key
    expand_row = iota((LANES, columns), 0)
    expand_key = third(iota((LANES, columns), 1) >> 2)
    expand = jnp.where(expand_row == expand_key, 1.0, 0.0).astype(BF16)
    spread = dot(small[...].astype(BF16), expand)
    mine = iota((ROWS, columns), 0) == col_tpl

    def flat(i):
        return jnp.sum(jnp.where(mine, spread[8 * i : 8 * i + 8], 0.0), axis=0, keepdims=True)

    owner_of, local_id, move_high, move_low = flat(0), flat(1), flat(2), flat(3)
    used = jnp.zeros((ROWS, columns), jnp.int32)
    for t in range(tpl_dev):
        used = jnp.where(col_tpl == t, station_count[t], used)
    live = (col_key < used) & (col < entries)
    owner_live = jnp.where(live[0:1], owner_of, -1.0)

    row = iota((rows_all, 1), 0)
    q = row & (BOX - 1)
    traced = q < channels * places
    row_place = jnp.where(traced, third(q), q - channels * places)
    row_chan = jnp.where(traced, q - channels * row_place, 0)
    row_rank = (row_place & 1).astype(F32)
    row_peer = ((row >> 4) + me) & (peers - 1)
    row_owner = (2 * row_peer + (row_place >> 1)).astype(F32)
    belongs = owner_live == row_owner
    up_row, up_col = iota((columns, columns), 0), iota((columns, columns), 1)
    up_chan = (up_row >> 2) - 3 * third(up_row >> 2)
    up_chan_col = (up_col >> 2) - 3 * third(up_col >> 2)
    earlier = jnp.where((up_row < up_col) & (up_chan == up_chan_col), 1.0, 0.0).astype(BF16)
    before = dot(jnp.where(belongs, 1.0, 0.0).astype(BF16), earlier)
    hot = jnp.where(
        belongs & (before == row_rank) & (col_chan[0:1] == row_chan), 1.0, 0.0
    )
    pick[...] = hot.astype(BF16)

    load_raw.wait()
    quads = raw[...].astype(F32).reshape(width * channels // 2, 2, tpl_dev, length)
    traces[...] = jnp.zeros(traces.shape, F32)
    traces[0 : width * channels // 2, 0:4, :] = quads[:, 0]
    traces[0 : width * channels // 2, 4:8, :] = quads[:, 1]
    placed = dot(pick[...], traces[...].reshape(columns, length).astype(BF16))
    ones = jnp.ones((columns, LANES), BF16)
    notes = jnp.concatenate(
        [dot((hot * v).astype(BF16), ones) for v in (local_id, move_high, move_low)], axis=1
    )
    outbox[...] = (
        jnp.where(traced, placed, notes).reshape(peers, BOX, length).astype(BF16)
    )

    def box_copy(i):
        return pltpu.make_async_remote_copy(
            src_ref=outbox.at[i],
            dst_ref=inbox.at[peers - i],
            send_sem=box_sem.at[0],
            recv_sem=box_sem.at[1],
            device_id=member(i),
            device_id_type=MESH,
        )

    def post(i, carry):
        box_copy(turn(i)).start()
        return carry

    keep = pltpu.make_async_copy(outbox.at[0], inbox.at[0], box_sem.at[2])
    keep.start()
    lax.fori_loop(0, peers - 1, post, 0)
    for k in relays:
        relay_copy(k).wait_recv()
        spread_part(k)

    order_row = iota((rows_all, 1), 0)
    group, inner = order_row // slots, order_row % slots
    place, sender = inner // peers, inner % peers
    at_row = jnp.where(group < channels, group + channels * place, channels * places + place)
    order = jnp.where(
        iota((rows_all, rows_all), 1) == sender * BOX + at_row, 1.0, 0.0
    ).astype(BF16)
    staged[...] = jnp.zeros(staged.shape, F32)
    load_offsets.wait()
    load_forward.wait()
    load_inverse.wait()
    load_band.wait()
    base = me * pair
    offset_row = jnp.sum(
        jnp.where(
            iota(offsets.shape, 0) == base // LANES, offsets[...].astype(F32), 0.0
        ),
        axis=0,
        keepdims=True,
    )

    keep.wait()
    others = pl.ds(1, peers - 1)
    pltpu.make_async_copy(outbox.at[others], inbox.at[others], box_sem.at[1]).wait()
    arrived = inbox[...].astype(F32).reshape(rows_all, length).astype(BF16)
    sorted_rows = dot(order, arrived)
    meta = sorted_rows[channels * slots :]
    lane = iota((slots, LANES), 1)
    block = iota((slots, LANES), 0) // (CAPACITY * peers)
    ids = meta[:, 0:LANES].astype(jnp.int32) + stations * block
    offset_hot = jnp.where(lane == ids + base % LANES, offset_row, 0.0).astype(BF16)
    offset_of = dot(offset_hot, jnp.ones((LANES, LANES), BF16))
    shift = (
        2.0 * meta[:, LANES : 2 * LANES] + meta[:, 2 * LANES : 3 * LANES] + offset_of
    ).astype(jnp.int32)
    station_hot = jnp.where(
        iota((slots, pair), 1) == ids[:, :pair], 1.0, 0.0
    ).astype(BF16)
    tracks = sorted_rows[: channels * slots]
    power = jnp.sum(tracks * tracks, axis=1, keepdims=True) * (1.0 / length)
    scale = lax.rsqrt(power + EPSILON)
    tspec = dot(tracks.astype(BF16), forward[0:length, :]) * scale

    wide = iota((4 * ROWS, columns), 0)
    wide_col = iota((4 * ROWS, columns), 1)
    of_template = jnp.where((wide & 7) == (wide_col & 3), 1.0, 0.0).astype(BF16)
    of_rows = lax.dot_general(
        of_template, pick[...], (((1,), (1,)), ((), ())), preferred_element_type=F32
    )
    weight_q = iota((4 * ROWS, rows_all), 1) & (BOX - 1)
    weight_j = iota((4 * ROWS, rows_all), 0) >> 3
    matches = (weight_q < span * places) & (weight_q - span * third(weight_q) == weight_j)
    of_rows = jnp.where(matches, of_rows, 0.0).astype(BF16)

    for i in range(2 * tpl):
        pltpu.make_async_copy(chunk_out, parts.at[i], part_recv.at[i]).wait()
    records = []
    for h in range(2):
        pieces = []
        for i in range(tpl):
            piece = parts[h * tpl + i].astype(F32)
            pieces += [piece[j * held : (j + 1) * held] for j in range(full)]
            tail = []
            for g in range(groups):
                at = full * held + g // per * ROWS
                tail.append(piece[at : at + ROWS, g % per * rest : (g % per + 1) * rest])
            pieces.append(jnp.concatenate(tail, axis=0))
        records.append(jnp.concatenate(pieces, axis=1))
    blocks = jnp.concatenate(
        [
            records[h][c * stations : (c + 1) * stations, b * length : b * length + frame]
            for b in range(2)
            for c in range(channels)
            for h in range(2)
        ],
        axis=0,
    )
    spectra = dot(blocks.astype(BF16), forward[...]).astype(BF16)
    energy = dot((blocks * blocks).astype(BF16), band[...])
    norm = (2.0 / (frame * length)) * lax.rsqrt(energy * (1.0 / length) + EPSILON)
    norm = norm.astype(BF16)

    def reply_copy(i):
        return pltpu.make_async_remote_copy(
            src_ref=replies.at[i],
            dst_ref=answers.at[peers - i],
            send_sem=back_sem.at[0],
            recv_sem=back_sem.at[1],
            device_id=member(i),
            device_id_type=MESH,
        )

    def answer(i, carry):
        reply_copy(turn(i)).start()
        return carry

    pairs = [(c, b) for b in range(2) for c in range(channels)]
    products, weights = [], []
    for c, b in pairs:
        at = slice((b * channels + c) * pair, (b * channels + c + 1) * pair)
        mine = slice(c * slots, (c + 1) * slots)
        y = tspec[mine]
        y_re, y_im = y[:, :length], y[:, length:]
        data = dot(station_hot, spectra[at])
        x_re, x_im = data[:, :length], data[:, length:]
        products.append(
            jnp.concatenate(
                [y_re * x_re + y_im * x_im, y_re * x_im - y_im * x_re], axis=1
            ).astype(BF16)
        )
        weights.append(dot(station_hot, norm[at]))
    lagged = dot(jnp.concatenate(products, axis=0), inverse[...])
    sums = [None, None]
    for n, (c, b) in enumerate(pairs):
        term = lagged[n * slots : (n + 1) * slots] * weights[n]
        sums[b] = term if c == 0 else sums[b] + term
    tiles = [sums[b][:, j * LANES : (j + 1) * LANES] for b in range(2) for j in range(span)]
    for bit in (2, 1):
        chosen = (shift & (bit * LANES)) != 0
        tiles = [
            jnp.where(chosen, tiles[min(i + bit, len(tiles) - 1)], tiles[i])
            for i in range(span + bit)
        ]
    step = LANES // 2
    while step >= 1:
        chosen = (shift & step) != 0
        turned = [pltpu.roll(tile, LANES - step, 1) for tile in tiles]
        inside = lane < LANES - step
        after = turned[1:] + turned[-1:]
        tiles = [
            jnp.where(chosen, jnp.where(inside, turned[i], after[i]), tiles[i])
            for i in range(span + 1)
        ]
        step //= 2
    for i in range(places):
        for j in range(span):
            staged[:, i * span + j, :] = tiles[j][i * peers : (i + 1) * peers]
    replies[...] = staged[...].astype(BF16)
    for j in range(peers - 1):
        answer(j, 0)
    keep_back = pltpu.make_async_copy(replies.at[0], answers.at[0], back_sem.at[2])
    keep_back.start()

    keep_back.wait()
    pltpu.make_async_copy(replies.at[others], answers.at[others], back_sem.at[1]).wait()
    stacked = dot(of_rows, answers[...].astype(F32).reshape(rows_all, LANES).astype(BF16))
    tops = [stacked[ROWS * j : ROWS * (j + 1)] for j in range(span)]
    square = tops[0] * tops[0]
    for top in tops[1:]:
        square = square + top * top
    mean = jnp.sum(square, axis=1, keepdims=True) * (1.0 / length)
    root = lax.rsqrt(mean + EPSILON)
    for j in range(span):
        out[:, j * LANES : (j + 1) * LANES] = tops[j] * root

    for k in range(len(ROUTES)):
        if k in relays:
            relay_copy(k).wait_send()
        for n in ROUTES[k][1]:
            if n:
                part_copy(k, n).wait_send()
                continue

            @pl.when(jnp.logical_not(stays(k)))
            def _():
                part_copy(k, n).wait_send()

    pltpu.make_async_copy(outbox.at[others], inbox.at[others], box_sem.at[0]).wait()
    pltpu.make_async_copy(replies.at[others], answers.at[others], back_sem.at[0]).wait()


def on_device(samples, templates, station_list, station_count, moveout, offsets):
    stations, channels, part = samples.shape
    tpl_dev, width, _, length = templates.shape
    tpl, sta = lax.axis_size("tpl"), lax.axis_size("sta")
    sizes = (tpl, sta, stations, channels, tpl_dev, width, length, part)
    held = stations * channels
    packs = -(-(held // ROWS) // (LANES // (part % LANES)))
    packed = part // LANES * held + ROWS * packs
    rows = jnp.transpose(samples, (1, 0, 2)).reshape(channels * stations, part)
    quads = jnp.transpose(templates, (1, 2, 0, 3)).reshape(width * channels, tpl_dev, length)
    offset_grid = offsets.reshape(-1, LANES)
    frame = 2 * length
    entries = tpl_dev * width * channels
    columns = (entries + LANES - 1) // LANES * LANES
    hbm = pl.BlockSpec(memory_space=pltpu.HBM)
    vmem = pl.BlockSpec(memory_space=pltpu.VMEM)
    dma = pltpu.SemaphoreType.DMA
    scaled = pl.pallas_call(
        functools.partial(kernel, sizes),
        out_shape=jax.ShapeDtypeStruct((ROWS, length), F32),
        in_specs=[hbm] * 9,
        out_specs=vmem,
        scratch_shapes=[
            pltpu.VMEM((frame, frame), BF16),
            pltpu.VMEM((frame, length), BF16),
            pltpu.VMEM((frame, length), BF16),
            pltpu.VMEM((width * channels, tpl_dev, length), BF16),
            pltpu.VMEM(station_list.shape, jnp.int32),
            pltpu.SMEM(station_count.shape, jnp.int32),
            pltpu.VMEM(moveout.shape, jnp.int32),
            pltpu.VMEM(offset_grid.shape, jnp.int32),
            pltpu.VMEM((columns // ROWS, ROWS, length), F32),
            pltpu.VMEM((4 * ROWS, LANES), F32),
            pltpu.VMEM((sta * ROWS, columns), BF16),
            pltpu.VMEM((held, part), BF16),
            pltpu.VMEM((packed, LANES), BF16),
            pltpu.VMEM((len(ROUTES), packed, LANES), BF16),
            pltpu.VMEM((sta // 2, BOX, length), BF16),
            pltpu.VMEM((sta // 2, BOX, length), BF16),
            pltpu.VMEM((2 * tpl, packed, LANES), BF16),
            pltpu.VMEM((sta // 2, BOX, LANES), F32),
            pltpu.VMEM((sta // 2, BOX, LANES), BF16),
            pltpu.VMEM((sta // 2, BOX, LANES), BF16),
            dma((9,)),
            dma((2 * tpl,)),
            dma((2 * tpl,)),
            dma((len(ROUTES),)),
            dma((len(ROUTES),)),
            dma((3,)),
            dma((3,)),
        ],
        compiler_params=pltpu.CompilerParams(
            collective_id=0, has_side_effects=True, vmem_limit_bytes=60 * 2**20
        ),
        cost_estimate=pl.CostEstimate(
            flops=2 * 10**9, bytes_accessed=6 * 10**6, transcendentals=10**5
        ),
    )(rows, quads, station_list, station_count, moveout, offset_grid, *tables(length))
    return scaled[:tpl_dev]


def solution(mesh):
    in_specs = (
        P("sta", None, "tpl"),
        P(("tpl", "sta"), None, None, None),
        P(("tpl", "sta"), None),
        P(("tpl", "sta")),
        P(("tpl", "sta"), None),
        P(),
    )
    out_specs = P(("tpl", "sta"), None)
    return jax.shard_map(
        on_device, mesh=mesh, in_specs=in_specs, out_specs=out_specs, check_vma=False
    )
```

```python
import functools
import math

import jax
import jax.numpy as jnp
import numpy as np
from jax import lax
from jax.experimental import pallas as pl
from jax.experimental.pallas import tpu as pltpu
from jax.sharding import PartitionSpec as P

EPSILON = 1e-06
LANES = 128
ROWS = 8
CAPACITY = 2
BOX = 16
TURN = 13
ROUTES = ((5, (3, 2, 1, 0, -1, -2)), (-5, (-2, -1, 0, 1, 2)), (0, (2, -2, 1, -1, 0)))
MESH = pl.DeviceIdType.MESH
F32 = jnp.float32
BF16 = jnp.bfloat16


def tables(length):
    frame = 2 * length
    time = np.arange(frame)
    odd = 2 * np.arange(length) + 1
    angles = (np.outer(time, odd) % (2 * frame)).astype(np.float64) * (math.pi / frame)
    cosine, sine = np.cos(angles), np.sin(angles)
    forward = np.concatenate([cosine, -sine], axis=1)
    inverse = np.concatenate([cosine[:length].T, -sine[:length].T], axis=0)
    row = np.arange(frame)[:, None]
    col = np.arange(length)[None, :]
    band = (row >= col) & (row < col + length)
    return tuple(jnp.asarray(a.astype(np.float32), BF16) for a in (forward, inverse, band))


def iota(shape, dim):
    return lax.broadcasted_iota(jnp.int32, shape, dim)


def dot(a, b):
    return jnp.dot(a, b, preferred_element_type=F32)


def third(value):
    return (value * 171) >> 9


def kernel(
    sizes,
    samples,
    templates,
    list_hbm,
    count_hbm,
    moveout_hbm,
    offsets_hbm,
    forward_hbm,
    inverse_hbm,
    band_hbm,
    out,
    forward,
    inverse,
    band,
    raw,
    station_list,
    station_count,
    moveout,
    offsets,
    traces,
    small,
    pick,
    chunk_in,
    chunk_out,
    relay,
    outbox,
    inbox,
    parts,
    staged,
    replies,
    answers,
    local_sem,
    part_send,
    part_recv,
    relay_send,
    relay_recv,
    box_sem,
    back_sem,
):
    tpl, sta, stations, channels, tpl_dev, width, length, part = sizes
    depth = 2 * tpl
    peers = sta // 2
    hops = [(k, n) for k, (far, near) in enumerate(ROUTES) for n in near]
    relays = [k for k, (far, near) in enumerate(ROUTES) if far]
    frame = 2 * length
    held = stations * channels
    pair = 2 * stations
    places = 2 * CAPACITY
    rows_all = peers * BOX
    slots = places * peers
    entries = tpl_dev * width * channels
    columns = (entries + LANES - 1) // LANES * LANES
    span = length // LANES

    p = lax.axis_index("tpl")
    s = lax.axis_index("sta")
    x, z = lax.div(s, depth), lax.rem(s, depth)
    me = x * tpl + p

    def turn(j):
        return (j + 1) * TURN % peers

    def member(i):
        d = lax.rem(me + i, peers)
        return {"tpl": lax.rem(d, tpl), "sta": lax.div(d, tpl) * depth + z}

    def plane(i):
        return x * depth + lax.rem(z + 2 * depth + i, depth)

    def load(n, src, dst):
        copy = pltpu.make_async_copy(src, dst, local_sem.at[n])
        copy.start()
        return copy

    load_chunk = load(8, samples, chunk_in)

    barrier = pltpu.get_barrier_semaphore()
    for k in relays:
        pl.semaphore_signal(
            barrier,
            inc=1,
            device_id={"tpl": p, "sta": plane(-ROUTES[k][0])},
            device_id_type=MESH,
        )
    for h in range(2):
        gap = lax.rem(z + depth - 2 * p - h, depth)
        hop = 0
        for k, n in hops:
            hop = jnp.where(gap == (ROUTES[k][0] + n) % depth, n, hop)

        @pl.when(hop != 0)
        def _():
            for i in range(tpl):
                pl.semaphore_signal(
                    barrier,
                    inc=1,
                    device_id={"tpl": i, "sta": plane(-hop)},
                    device_id_type=MESH,
                )

    def greet(i, carry):
        pl.semaphore_signal(
            barrier, inc=1, device_id=member(turn(i)), device_id_type=MESH
        )
        return carry

    for j in range(peers - 1):
        greet(j, 0)

    load_list = load(4, list_hbm, station_list)
    load_count = load(5, count_hbm, station_count)
    load_moveout = load(6, moveout_hbm, moveout)
    load_raw = load(0, templates, raw)
    load_offsets = load(7, offsets_hbm, offsets)
    load_forward = load(1, forward_hbm, forward)
    load_inverse = load(3, inverse_hbm, inverse)
    load_band = load(2, band_hbm, band)

    full, rest = part // LANES, part % LANES
    per = LANES // rest
    groups = held // ROWS
    load_chunk.wait()
    chunk = chunk_in[...].astype(F32)
    packed = [chunk[:, j * LANES : (j + 1) * LANES] for j in range(full)]
    for first in range(0, groups, per):
        pieces = [
            chunk[g * ROWS : (g + 1) * ROWS, full * LANES :]
            for g in range(first, min(first + per, groups))
        ]
        if len(pieces) < per:
            pieces.append(jnp.zeros((ROWS, (per - len(pieces)) * rest), F32))
        packed.append(jnp.concatenate(pieces, axis=1))
    chunk_out[...] = jnp.concatenate(packed, axis=0).astype(BF16)

    pl.semaphore_wait(barrier, peers - 1 + len(relays) + sum(n != 0 for k, n in hops))

    def relay_copy(k):
        return pltpu.make_async_remote_copy(
            src_ref=chunk_out,
            dst_ref=relay.at[k],
            send_sem=relay_send.at[k],
            recv_sem=relay_recv.at[k],
            device_id={"tpl": p, "sta": plane(ROUTES[k][0])},
            device_id_type=MESH,
        )

    def part_copy(k, n):
        origin = lax.rem(z + 2 * depth - ROUTES[k][0], depth)
        return pltpu.make_async_remote_copy(
            src_ref=relay.at[k] if ROUTES[k][0] else chunk_out,
            dst_ref=parts.at[lax.rem(origin, 2) * tpl + p],
            send_sem=part_send.at[hops.index((k, n))],
            recv_sem=part_recv.at[lax.rem(origin, 2) * tpl + p],
            device_id={"tpl": lax.div(origin, 2), "sta": plane(n)},
            device_id_type=MESH,
        )

    def stays(k):
        return lax.rem(z + 2 * depth - ROUTES[k][0], depth) // 2 == p

    def spread_part(k):
        for n in ROUTES[k][1]:
            if n:
                part_copy(k, n).start()
                continue

            @pl.when(jnp.logical_not(stays(k)))
            def _():
                part_copy(k, n).start()

            @pl.when(stays(k))
            def _():
                origin = lax.rem(z + 2 * depth - ROUTES[k][0], depth)
                place = lax.rem(origin, 2) * tpl + p
                pltpu.make_async_copy(
                    relay.at[k] if ROUTES[k][0] else chunk_out, parts.at[place], part_recv.at[place]
                ).start()

    for k in relays:
        relay_copy(k).start()
    for k in range(len(ROUTES)):
        if k not in relays:
            spread_part(k)

    small[...] = jnp.zeros(small.shape, F32)
    load_list.wait()
    load_count.wait()
    load_moveout.wait()
    stations_here = station_list[...]
    moves = moveout[...]
    small[0:tpl_dev, 0:width] = (stations_here >> 4).astype(F32)
    small[8 : 8 + tpl_dev, 0:width] = (stations_here & 15).astype(F32)
    small[16 : 16 + tpl_dev, 0:width] = (moves >> 1).astype(F32)
    small[24 : 24 + tpl_dev, 0:width] = (moves & 1).astype(F32)
    col = iota((ROWS, columns), 1)
    col_tpl = col & 3
    col_key = third(col >> 2)
    col_chan = (col >> 2) - 3 * col_key
    expand_row = iota((LANES, columns), 0)
    expand_key = third(iota((LANES, columns), 1) >> 2)
    expand = jnp.where(expand_row == expand_key, 1.0, 0.0).astype(BF16)
    spread = dot(small[...].astype(BF16), expand)
    mine = iota((ROWS, columns), 0) == col_tpl

    def flat(i):
        return jnp.sum(jnp.where(mine, spread[8 * i : 8 * i + 8], 0.0), axis=0, keepdims=True)

    owner_of, local_id, move_high, move_low = flat(0), flat(1), flat(2), flat(3)
    used = jnp.zeros((ROWS, columns), jnp.int32)
    for t in range(tpl_dev):
        used = jnp.where(col_tpl == t, station_count[t], used)
    live = (col_key < used) & (col < entries)
    owner_live = jnp.where(live[0:1], owner_of, -1.0)

    row = iota((rows_all, 1), 0)
    q = row & (BOX - 1)
    traced = q < channels * places
    row_place = jnp.where(traced, third(q), q - channels * places)
    row_chan = jnp.where(traced, q - channels * row_place, 0)
    row_rank = (row_place & 1).astype(F32)
    row_peer = ((row >> 4) + me) & (peers - 1)
    row_owner = (2 * row_peer + (row_place >> 1)).astype(F32)
    belongs = owner_live == row_owner
    up_row, up_col = iota((columns, columns), 0), iota((columns, columns), 1)
    up_chan = (up_row >> 2) - 3 * third(up_row >> 2)
    up_chan_col = (up_col >> 2) - 3 * third(up_col >> 2)
    earlier = jnp.where((up_row < up_col) & (up_chan == up_chan_col), 1.0, 0.0).astype(BF16)
    before = dot(jnp.where(belongs, 1.0, 0.0).astype(BF16), earlier)
    hot = jnp.where(
        belongs & (before == row_rank) & (col_chan[0:1] == row_chan), 1.0, 0.0
    )
    pick[...] = hot.astype(BF16)

    load_raw.wait()
    quads = raw[...].astype(F32).reshape(width * channels // 2, 2, tpl_dev, length)
    traces[...] = jnp.zeros(traces.shape, F32)
    traces[0 : width * channels // 2, 0:4, :] = quads[:, 0]
    traces[0 : width * channels // 2, 4:8, :] = quads[:, 1]
    placed = dot(pick[...], traces[...].reshape(columns, length).astype(BF16))
    ones = jnp.ones((columns, LANES), BF16)
    notes = jnp.concatenate(
        [dot((hot * v).astype(BF16), ones) for v in (local_id, move_high, move_low)], axis=1
    )
    outbox[...] = (
        jnp.where(traced, placed, notes).reshape(peers, BOX, length).astype(BF16)
    )

    def box_copy(i):
        return pltpu.make_async_remote_copy(
            src_ref=outbox.at[i],
            dst_ref=inbox.at[peers - i],
            send_sem=box_sem.at[0],
            recv_sem=box_sem.at[1],
            device_id=member(i),
            device_id_type=MESH,
        )

    def post(i, carry):
        box_copy(turn(i)).start()
        return carry

    keep = pltpu.make_async_copy(outbox.at[0], inbox.at[0], box_sem.at[2])
    keep.start()
    for j in range(peers - 1):
        post(j, 0)
    for k in relays:
        relay_copy(k).wait_recv()
        spread_part(k)

    order_row = iota((rows_all, 1), 0)
    group, inner = order_row // slots, order_row % slots
    place, sender = inner // peers, inner % peers
    at_row = jnp.where(group < channels, group + channels * place, channels * places + place)
    order = jnp.where(
        iota((rows_all, rows_all), 1) == sender * BOX + at_row, 1.0, 0.0
    ).astype(BF16)
    staged[...] = jnp.zeros(staged.shape, F32)
    load_offsets.wait()
    load_forward.wait()
    load_inverse.wait()
    load_band.wait()
    base = me * pair
    offset_row = jnp.sum(
        jnp.where(
            iota(offsets.shape, 0) == base // LANES, offsets[...].astype(F32), 0.0
        ),
        axis=0,
        keepdims=True,
    )

    keep.wait()
    others = pl.ds(1, peers - 1)
    pltpu.make_async_copy(outbox.at[others], inbox.at[others], box_sem.at[1]).wait()
    arrived = inbox[...].astype(F32).reshape(rows_all, length).astype(BF16)
    sorted_rows = dot(order, arrived)
    meta = sorted_rows[channels * slots :]
    lane = iota((slots, LANES), 1)
    block = iota((slots, LANES), 0) // (CAPACITY * peers)
    ids = meta[:, 0:LANES].astype(jnp.int32) + stations * block
    offset_hot = jnp.where(lane == ids + base % LANES, offset_row, 0.0).astype(BF16)
    offset_of = dot(offset_hot, jnp.ones((LANES, LANES), BF16))
    shift = (
        2.0 * meta[:, LANES : 2 * LANES] + meta[:, 2 * LANES : 3 * LANES] + offset_of
    ).astype(jnp.int32)
    station_hot = jnp.where(
        iota((slots, pair), 1) == ids[:, :pair], 1.0, 0.0
    ).astype(BF16)
    tracks = sorted_rows[: channels * slots]
    power = jnp.sum(tracks * tracks, axis=1, keepdims=True) * (1.0 / length)
    scale = lax.rsqrt(power + EPSILON)
    tspec = dot(tracks.astype(BF16), forward[0:length, :]) * scale

    wide = iota((4 * ROWS, columns), 0)
    wide_col = iota((4 * ROWS, columns), 1)
    of_template = jnp.where((wide & 7) == (wide_col & 3), 1.0, 0.0).astype(BF16)
    of_rows = lax.dot_general(
        of_template, pick[...], (((1,), (1,)), ((), ())), preferred_element_type=F32
    )
    weight_q = iota((4 * ROWS, rows_all), 1) & (BOX - 1)
    weight_j = iota((4 * ROWS, rows_all), 0) >> 3
    matches = (weight_q < span * places) & (weight_q - span * third(weight_q) == weight_j)
    of_rows = jnp.where(matches, of_rows, 0.0).astype(BF16)

    for i in range(2 * tpl):
        pltpu.make_async_copy(chunk_out, parts.at[i], part_recv.at[i]).wait()
    records = []
    for h in range(2):
        pieces = []
        for i in range(tpl):
            piece = parts[h * tpl + i].astype(F32)
            pieces += [piece[j * held : (j + 1) * held] for j in range(full)]
            tail = []
            for g in range(groups):
                at = full * held + g // per * ROWS
                tail.append(piece[at : at + ROWS, g % per * rest : (g % per + 1) * rest])
            pieces.append(jnp.concatenate(tail, axis=0))
        records.append(jnp.concatenate(pieces, axis=1))
    blocks = jnp.concatenate(
        [
            records[h][c * stations : (c + 1) * stations, b * length : b * length + frame]
            for b in range(2)
            for c in range(channels)
            for h in range(2)
        ],
        axis=0,
    )
    spectra = dot(blocks.astype(BF16), forward[...]).astype(BF16)
    energy = dot((blocks * blocks).astype(BF16), band[...])
    norm = (2.0 / (frame * length)) * lax.rsqrt(energy * (1.0 / length) + EPSILON)
    norm = norm.astype(BF16)

    def reply_copy(i):
        return pltpu.make_async_remote_copy(
            src_ref=replies.at[i],
            dst_ref=answers.at[peers - i],
            send_sem=back_sem.at[0],
            recv_sem=back_sem.at[1],
            device_id=member(i),
            device_id_type=MESH,
        )

    def answer(i, carry):
        reply_copy(turn(i)).start()
        return carry

    pairs = [(c, b) for b in range(2) for c in range(channels)]
    products, weights = [], []
    for c, b in pairs:
        at = slice((b * channels + c) * pair, (b * channels + c + 1) * pair)
        mine = slice(c * slots, (c + 1) * slots)
        y = tspec[mine]
        y_re, y_im = y[:, :length], y[:, length:]
        data = dot(station_hot, spectra[at])
        x_re, x_im = data[:, :length], data[:, length:]
        products.append(
            jnp.concatenate(
                [y_re * x_re + y_im * x_im, y_re * x_im - y_im * x_re], axis=1
            ).astype(BF16)
        )
        weights.append(dot(station_hot, norm[at]))
    lagged = dot(jnp.concatenate(products, axis=0), inverse[...])
    sums = [None, None]
    for n, (c, b) in enumerate(pairs):
        term = lagged[n * slots : (n + 1) * slots] * weights[n]
        sums[b] = term if c == 0 else sums[b] + term
    tiles = [sums[b][:, j * LANES : (j + 1) * LANES] for b in range(2) for j in range(span)]
    for bit in (2, 1):
        chosen = (shift & (bit * LANES)) != 0
        tiles = [
            jnp.where(chosen, tiles[min(i + bit, len(tiles) - 1)], tiles[i])
            for i in range(span + bit)
        ]
    step = LANES // 2
    while step >= 1:
        chosen = (shift & step) != 0
        turned = [pltpu.roll(tile, LANES - step, 1) for tile in tiles]
        inside = lane < LANES - step
        after = turned[1:] + turned[-1:]
        tiles = [
            jnp.where(chosen, jnp.where(inside, turned[i], after[i]), tiles[i])
            for i in range(span + 1)
        ]
        step //= 2
    for i in range(places):
        for j in range(span):
            staged[:, i * span + j, :] = tiles[j][i * peers : (i + 1) * peers]
    replies[...] = staged[...].astype(BF16)
    for j in range(peers - 1):
        answer(j, 0)
    keep_back = pltpu.make_async_copy(replies.at[0], answers.at[0], back_sem.at[2])
    keep_back.start()

    keep_back.wait()
    pltpu.make_async_copy(replies.at[others], answers.at[others], back_sem.at[1]).wait()
    stacked = dot(of_rows, answers[...].astype(F32).reshape(rows_all, LANES).astype(BF16))
    tops = [stacked[ROWS * j : ROWS * (j + 1)] for j in range(span)]
    square = tops[0] * tops[0]
    for top in tops[1:]:
        square = square + top * top
    mean = jnp.sum(square, axis=1, keepdims=True) * (1.0 / length)
    root = lax.rsqrt(mean + EPSILON)
    for j in range(span):
        out[:, j * LANES : (j + 1) * LANES] = tops[j] * root

    for k in range(len(ROUTES)):
        if k in relays:
            relay_copy(k).wait_send()
        for n in ROUTES[k][1]:
            if n:
                part_copy(k, n).wait_send()
                continue

            @pl.when(jnp.logical_not(stays(k)))
            def _():
                part_copy(k, n).wait_send()

    pltpu.make_async_copy(outbox.at[others], inbox.at[others], box_sem.at[0]).wait()
    pltpu.make_async_copy(replies.at[others], answers.at[others], back_sem.at[0]).wait()


def on_device(samples, templates, station_list, station_count, moveout, offsets):
    stations, channels, part = samples.shape
    tpl_dev, width, _, length = templates.shape
    tpl, sta = lax.axis_size("tpl"), lax.axis_size("sta")
    sizes = (tpl, sta, stations, channels, tpl_dev, width, length, part)
    held = stations * channels
    packs = -(-(held // ROWS) // (LANES // (part % LANES)))
    packed = part // LANES * held + ROWS * packs
    rows = jnp.transpose(samples, (1, 0, 2)).reshape(channels * stations, part)
    quads = jnp.transpose(templates, (1, 2, 0, 3)).reshape(width * channels, tpl_dev, length)
    offset_grid = offsets.reshape(-1, LANES)
    frame = 2 * length
    entries = tpl_dev * width * channels
    columns = (entries + LANES - 1) // LANES * LANES
    hbm = pl.BlockSpec(memory_space=pltpu.HBM)
    vmem = pl.BlockSpec(memory_space=pltpu.VMEM)
    dma = pltpu.SemaphoreType.DMA
    scaled = pl.pallas_call(
        functools.partial(kernel, sizes),
        out_shape=jax.ShapeDtypeStruct((ROWS, length), F32),
        in_specs=[hbm] * 9,
        out_specs=vmem,
        scratch_shapes=[
            pltpu.VMEM((frame, frame), BF16),
            pltpu.VMEM((frame, length), BF16),
            pltpu.VMEM((frame, length), BF16),
            pltpu.VMEM((width * channels, tpl_dev, length), BF16),
            pltpu.VMEM(station_list.shape, jnp.int32),
            pltpu.SMEM(station_count.shape, jnp.int32),
            pltpu.VMEM(moveout.shape, jnp.int32),
            pltpu.VMEM(offset_grid.shape, jnp.int32),
            pltpu.VMEM((columns // ROWS, ROWS, length), F32),
            pltpu.VMEM((4 * ROWS, LANES), F32),
            pltpu.VMEM((sta * ROWS, columns), BF16),
            pltpu.VMEM((held, part), BF16),
            pltpu.VMEM((packed, LANES), BF16),
            pltpu.VMEM((len(ROUTES), packed, LANES), BF16),
            pltpu.VMEM((sta // 2, BOX, length), BF16),
            pltpu.VMEM((sta // 2, BOX, length), BF16),
            pltpu.VMEM((2 * tpl, packed, LANES), BF16),
            pltpu.VMEM((sta // 2, BOX, LANES), F32),
            pltpu.VMEM((sta // 2, BOX, LANES), BF16),
            pltpu.VMEM((sta // 2, BOX, LANES), BF16),
            dma((9,)),
            dma((2 * tpl,)),
            dma((2 * tpl,)),
            dma((len(ROUTES),)),
            dma((len(ROUTES),)),
            dma((3,)),
            dma((3,)),
        ],
        compiler_params=pltpu.CompilerParams(
            collective_id=0, has_side_effects=True, vmem_limit_bytes=60 * 2**20
        ),
        cost_estimate=pl.CostEstimate(
            flops=2 * 10**9, bytes_accessed=6 * 10**6, transcendentals=10**5
        ),
    )(rows, quads, station_list, station_count, moveout, offset_grid, *tables(length))
    return scaled[:tpl_dev]


def solution(mesh):
    in_specs = (
        P("sta", None, "tpl"),
        P(("tpl", "sta"), None, None, None),
        P(("tpl", "sta"), None),
        P(("tpl", "sta")),
        P(("tpl", "sta"), None),
        P(),
    )
    out_specs = P(("tpl", "sta"), None)
    return jax.shard_map(
        on_device, mesh=mesh, in_specs=in_specs, out_specs=out_specs, check_vma=False
    )
```

```python
import functools
import math

import jax
import jax.numpy as jnp
import numpy as np
from jax import lax
from jax.experimental import pallas as pl
from jax.experimental.pallas import tpu as pltpu
from jax.sharding import PartitionSpec as P

EPSILON = 1e-06
LANES = 128
ROWS = 8
CAPACITY = 2
BOX = 16
TURN = 13
ROUTES = ((4, (4, 3, 2, 1, 0, -1)), (-4, (-3, -2, -1, 0, 1)), (0, (2, -2, 1, -1, 0)))
MESH = pl.DeviceIdType.MESH
F32 = jnp.float32
BF16 = jnp.bfloat16


def tables(length):
    frame = 2 * length
    time = np.arange(frame)
    odd = 2 * np.arange(length) + 1
    angles = (np.outer(time, odd) % (2 * frame)).astype(np.float64) * (math.pi / frame)
    cosine, sine = np.cos(angles), np.sin(angles)
    forward = np.concatenate([cosine, -sine], axis=1)
    inverse = np.concatenate([cosine[:length].T, -sine[:length].T], axis=0)
    row = np.arange(frame)[:, None]
    col = np.arange(length)[None, :]
    band = (row >= col) & (row < col + length)
    return tuple(jnp.asarray(a.astype(np.float32), BF16) for a in (forward, inverse, band))


def iota(shape, dim):
    return lax.broadcasted_iota(jnp.int32, shape, dim)


def dot(a, b):
    return jnp.dot(a, b, preferred_element_type=F32)


def third(value):
    return (value * 171) >> 9


def kernel(
    sizes,
    samples,
    templates,
    list_hbm,
    count_hbm,
    moveout_hbm,
    offsets_hbm,
    forward_hbm,
    inverse_hbm,
    band_hbm,
    out,
    forward,
    inverse,
    band,
    raw,
    station_list,
    station_count,
    moveout,
    offsets,
    traces,
    small,
    pick,
    chunk_in,
    chunk_out,
    relay,
    outbox,
    inbox,
    parts,
    staged,
    replies,
    answers,
    local_sem,
    part_send,
    part_recv,
    relay_send,
    relay_recv,
    box_sem,
    back_sem,
):
    tpl, sta, stations, channels, tpl_dev, width, length, part = sizes
    depth = 2 * tpl
    peers = sta // 2
    hops = [(k, n) for k, (far, near) in enumerate(ROUTES) for n in near]
    relays = [k for k, (far, near) in enumerate(ROUTES) if far]
    frame = 2 * length
    held = stations * channels
    pair = 2 * stations
    places = 2 * CAPACITY
    rows_all = peers * BOX
    slots = places * peers
    entries = tpl_dev * width * channels
    columns = (entries + LANES - 1) // LANES * LANES
    span = length // LANES

    p = lax.axis_index("tpl")
    s = lax.axis_index("sta")
    x, z = lax.div(s, depth), lax.rem(s, depth)
    me = x * tpl + p

    def turn(j):
        return (j + 1) * TURN % peers

    def member(i):
        d = lax.rem(me + i, peers)
        return {"tpl": lax.rem(d, tpl), "sta": lax.div(d, tpl) * depth + z}

    def plane(i):
        return x * depth + lax.rem(z + 2 * depth + i, depth)

    def load(n, src, dst):
        copy = pltpu.make_async_copy(src, dst, local_sem.at[n])
        copy.start()
        return copy

    load_chunk = load(8, samples, chunk_in)

    barrier = pltpu.get_barrier_semaphore()
    for k in relays:
        pl.semaphore_signal(
            barrier,
            inc=1,
            device_id={"tpl": p, "sta": plane(-ROUTES[k][0])},
            device_id_type=MESH,
        )
    for h in range(2):
        gap = lax.rem(z + depth - 2 * p - h, depth)
        hop = 0
        for k, n in hops:
            hop = jnp.where(gap == (ROUTES[k][0] + n) % depth, n, hop)

        @pl.when(hop != 0)
        def _():
            for i in range(tpl):
                pl.semaphore_signal(
                    barrier,
                    inc=1,
                    device_id={"tpl": i, "sta": plane(-hop)},
                    device_id_type=MESH,
                )

    def greet(i, carry):
        pl.semaphore_signal(
            barrier, inc=1, device_id=member(turn(i)), device_id_type=MESH
        )
        return carry

    for j in range(peers - 1):
        greet(j, 0)

    load_list = load(4, list_hbm, station_list)
    load_count = load(5, count_hbm, station_count)
    load_moveout = load(6, moveout_hbm, moveout)
    load_raw = load(0, templates, raw)
    load_offsets = load(7, offsets_hbm, offsets)
    load_forward = load(1, forward_hbm, forward)
    load_inverse = load(3, inverse_hbm, inverse)
    load_band = load(2, band_hbm, band)

    full, rest = part // LANES, part % LANES
    per = LANES // rest
    groups = held // ROWS
    load_chunk.wait()
    chunk = chunk_in[...].astype(F32)
    packed = [chunk[:, j * LANES : (j + 1) * LANES] for j in range(full)]
    for first in range(0, groups, per):
        pieces = [
            chunk[g * ROWS : (g + 1) * ROWS, full * LANES :]
            for g in range(first, min(first + per, groups))
        ]
        if len(pieces) < per:
            pieces.append(jnp.zeros((ROWS, (per - len(pieces)) * rest), F32))
        packed.append(jnp.concatenate(pieces, axis=1))
    chunk_out[...] = jnp.concatenate(packed, axis=0).astype(BF16)

    pl.semaphore_wait(barrier, peers - 1 + len(relays) + sum(n != 0 for k, n in hops))

    def relay_copy(k):
        return pltpu.make_async_remote_copy(
            src_ref=chunk_out,
            dst_ref=relay.at[k],
            send_sem=relay_send.at[k],
            recv_sem=relay_recv.at[k],
            device_id={"tpl": p, "sta": plane(ROUTES[k][0])},
            device_id_type=MESH,
        )

    def part_copy(k, n):
        origin = lax.rem(z + 2 * depth - ROUTES[k][0], depth)
        return pltpu.make_async_remote_copy(
            src_ref=relay.at[k] if ROUTES[k][0] else chunk_out,
            dst_ref=parts.at[lax.rem(origin, 2) * tpl + p],
            send_sem=part_send.at[hops.index((k, n))],
            recv_sem=part_recv.at[lax.rem(origin, 2) * tpl + p],
            device_id={"tpl": lax.div(origin, 2), "sta": plane(n)},
            device_id_type=MESH,
        )

    def stays(k):
        return lax.rem(z + 2 * depth - ROUTES[k][0], depth) // 2 == p

    def spread_part(k):
        for n in ROUTES[k][1]:
            if n:
                part_copy(k, n).start()
                continue

            @pl.when(jnp.logical_not(stays(k)))
            def _():
                part_copy(k, n).start()

            @pl.when(stays(k))
            def _():
                origin = lax.rem(z + 2 * depth - ROUTES[k][0], depth)
                place = lax.rem(origin, 2) * tpl + p
                pltpu.make_async_copy(
                    relay.at[k] if ROUTES[k][0] else chunk_out, parts.at[place], part_recv.at[place]
                ).start()

    for k in relays:
        relay_copy(k).start()
    for k in range(len(ROUTES)):
        if k not in relays:
            spread_part(k)

    small[...] = jnp.zeros(small.shape, F32)
    load_list.wait()
    load_count.wait()
    load_moveout.wait()
    stations_here = station_list[...]
    moves = moveout[...]
    small[0:tpl_dev, 0:width] = (stations_here >> 4).astype(F32)
    small[8 : 8 + tpl_dev, 0:width] = (stations_here & 15).astype(F32)
    small[16 : 16 + tpl_dev, 0:width] = (moves >> 1).astype(F32)
    small[24 : 24 + tpl_dev, 0:width] = (moves & 1).astype(F32)
    col = iota((ROWS, columns), 1)
    col_tpl = col & 3
    col_key = third(col >> 2)
    col_chan = (col >> 2) - 3 * col_key
    expand_row = iota((LANES, columns), 0)
    expand_key = third(iota((LANES, columns), 1) >> 2)
    expand = jnp.where(expand_row == expand_key, 1.0, 0.0).astype(BF16)
    spread = dot(small[...].astype(BF16), expand)
    mine = iota((ROWS, columns), 0) == col_tpl

    def flat(i):
        return jnp.sum(jnp.where(mine, spread[8 * i : 8 * i + 8], 0.0), axis=0, keepdims=True)

    owner_of, local_id, move_high, move_low = flat(0), flat(1), flat(2), flat(3)
    used = jnp.zeros((ROWS, columns), jnp.int32)
    for t in range(tpl_dev):
        used = jnp.where(col_tpl == t, station_count[t], used)
    live = (col_key < used) & (col < entries)
    owner_live = jnp.where(live[0:1], owner_of, -1.0)

    row = iota((rows_all, 1), 0)
    q = row & (BOX - 1)
    traced = q < channels * places
    row_place = jnp.where(traced, third(q), q - channels * places)
    row_chan = jnp.where(traced, q - channels * row_place, 0)
    row_rank = (row_place & 1).astype(F32)
    row_peer = ((row >> 4) + me) & (peers - 1)
    row_owner = (2 * row_peer + (row_place >> 1)).astype(F32)
    belongs = owner_live == row_owner
    up_row, up_col = iota((columns, columns), 0), iota((columns, columns), 1)
    up_chan = (up_row >> 2) - 3 * third(up_row >> 2)
    up_chan_col = (up_col >> 2) - 3 * third(up_col >> 2)
    earlier = jnp.where((up_row < up_col) & (up_chan == up_chan_col), 1.0, 0.0).astype(BF16)
    before = dot(jnp.where(belongs, 1.0, 0.0).astype(BF16), earlier)
    hot = jnp.where(
        belongs & (before == row_rank) & (col_chan[0:1] == row_chan), 1.0, 0.0
    )
    pick[...] = hot.astype(BF16)

    load_raw.wait()
    quads = raw[...].astype(F32).reshape(width * channels // 2, 2, tpl_dev, length)
    traces[...] = jnp.zeros(traces.shape, F32)
    traces[0 : width * channels // 2, 0:4, :] = quads[:, 0]
    traces[0 : width * channels // 2, 4:8, :] = quads[:, 1]
    placed = dot(pick[...], traces[...].reshape(columns, length).astype(BF16))
    ones = jnp.ones((columns, LANES), BF16)
    notes = jnp.concatenate(
        [dot((hot * v).astype(BF16), ones) for v in (local_id, move_high, move_low)], axis=1
    )
    outbox[...] = (
        jnp.where(traced, placed, notes).reshape(peers, BOX, length).astype(BF16)
    )

    def box_copy(i):
        return pltpu.make_async_remote_copy(
            src_ref=outbox.at[i],
            dst_ref=inbox.at[peers - i],
            send_sem=box_sem.at[0],
            recv_sem=box_sem.at[1],
            device_id=member(i),
            device_id_type=MESH,
        )

    def post(i, carry):
        box_copy(turn(i)).start()
        return carry

    keep = pltpu.make_async_copy(outbox.at[0], inbox.at[0], box_sem.at[2])
    keep.start()
    for j in range(peers - 1):
        post(j, 0)
    for k in relays:
        relay_copy(k).wait_recv()
        spread_part(k)

    order_row = iota((rows_all, 1), 0)
    group, inner = order_row // slots, order_row % slots
    place, sender = inner // peers, inner % peers
    at_row = jnp.where(group < channels, group + channels * place, channels * places + place)
    order = jnp.where(
        iota((rows_all, rows_all), 1) == sender * BOX + at_row, 1.0, 0.0
    ).astype(BF16)
    staged[...] = jnp.zeros(staged.shape, F32)
    load_offsets.wait()
    load_forward.wait()
    load_inverse.wait()
    load_band.wait()
    base = me * pair
    offset_row = jnp.sum(
        jnp.where(
            iota(offsets.shape, 0) == base // LANES, offsets[...].astype(F32), 0.0
        ),
        axis=0,
        keepdims=True,
    )

    keep.wait()
    others = pl.ds(1, peers - 1)
    pltpu.make_async_copy(outbox.at[others], inbox.at[others], box_sem.at[1]).wait()
    arrived = inbox[...].astype(F32).reshape(rows_all, length).astype(BF16)
    sorted_rows = dot(order, arrived)
    meta = sorted_rows[channels * slots :]
    lane = iota((slots, LANES), 1)
    block = iota((slots, LANES), 0) // (CAPACITY * peers)
    ids = meta[:, 0:LANES].astype(jnp.int32) + stations * block
    offset_hot = jnp.where(lane == ids + base % LANES, offset_row, 0.0).astype(BF16)
    offset_of = dot(offset_hot, jnp.ones((LANES, LANES), BF16))
    shift = (
        2.0 * meta[:, LANES : 2 * LANES] + meta[:, 2 * LANES : 3 * LANES] + offset_of
    ).astype(jnp.int32)
    station_hot = jnp.where(
        iota((slots, pair), 1) == ids[:, :pair], 1.0, 0.0
    ).astype(BF16)
    tracks = sorted_rows[: channels * slots]
    power = jnp.sum(tracks * tracks, axis=1, keepdims=True) * (1.0 / length)
    scale = lax.rsqrt(power + EPSILON)
    tspec = dot(tracks.astype(BF16), forward[0:length, :]) * scale

    wide = iota((4 * ROWS, columns), 0)
    wide_col = iota((4 * ROWS, columns), 1)
    of_template = jnp.where((wide & 7) == (wide_col & 3), 1.0, 0.0).astype(BF16)
    of_rows = lax.dot_general(
        of_template, pick[...], (((1,), (1,)), ((), ())), preferred_element_type=F32
    )
    weight_q = iota((4 * ROWS, rows_all), 1) & (BOX - 1)
    weight_j = iota((4 * ROWS, rows_all), 0) >> 3
    matches = (weight_q < span * places) & (weight_q - span * third(weight_q) == weight_j)
    of_rows = jnp.where(matches, of_rows, 0.0).astype(BF16)

    for i in range(2 * tpl):
        pltpu.make_async_copy(chunk_out, parts.at[i], part_recv.at[i]).wait()
    records = []
    for h in range(2):
        pieces = []
        for i in range(tpl):
            piece = parts[h * tpl + i].astype(F32)
            pieces += [piece[j * held : (j + 1) * held] for j in range(full)]
            tail = []
            for g in range(groups):
                at = full * held + g // per * ROWS
                tail.append(piece[at : at + ROWS, g % per * rest : (g % per + 1) * rest])
            pieces.append(jnp.concatenate(tail, axis=0))
        records.append(jnp.concatenate(pieces, axis=1))
    blocks = jnp.concatenate(
        [
            records[h][c * stations : (c + 1) * stations, b * length : b * length + frame]
            for b in range(2)
            for c in range(channels)
            for h in range(2)
        ],
        axis=0,
    )
    spectra = dot(blocks.astype(BF16), forward[...]).astype(BF16)
    energy = dot((blocks * blocks).astype(BF16), band[...])
    norm = (2.0 / (frame * length)) * lax.rsqrt(energy * (1.0 / length) + EPSILON)
    norm = norm.astype(BF16)

    def reply_copy(i):
        return pltpu.make_async_remote_copy(
            src_ref=replies.at[i],
            dst_ref=answers.at[peers - i],
            send_sem=back_sem.at[0],
            recv_sem=back_sem.at[1],
            device_id=member(i),
            device_id_type=MESH,
        )

    def answer(i, carry):
        reply_copy(turn(i)).start()
        return carry

    pairs = [(c, b) for b in range(2) for c in range(channels)]
    products, weights = [], []
    for c, b in pairs:
        at = slice((b * channels + c) * pair, (b * channels + c + 1) * pair)
        mine = slice(c * slots, (c + 1) * slots)
        y = tspec[mine]
        y_re, y_im = y[:, :length], y[:, length:]
        data = dot(station_hot, spectra[at])
        x_re, x_im = data[:, :length], data[:, length:]
        products.append(
            jnp.concatenate(
                [y_re * x_re + y_im * x_im, y_re * x_im - y_im * x_re], axis=1
            ).astype(BF16)
        )
        weights.append(dot(station_hot, norm[at]))
    lagged = dot(jnp.concatenate(products, axis=0), inverse[...])
    sums = [None, None]
    for n, (c, b) in enumerate(pairs):
        term = lagged[n * slots : (n + 1) * slots] * weights[n]
        sums[b] = term if c == 0 else sums[b] + term
    tiles = [sums[b][:, j * LANES : (j + 1) * LANES] for b in range(2) for j in range(span)]
    for bit in (2, 1):
        chosen = (shift & (bit * LANES)) != 0
        tiles = [
            jnp.where(chosen, tiles[min(i + bit, len(tiles) - 1)], tiles[i])
            for i in range(span + bit)
        ]
    step = LANES // 2
    while step >= 1:
        chosen = (shift & step) != 0
        turned = [pltpu.roll(tile, LANES - step, 1) for tile in tiles]
        inside = lane < LANES - step
        after = turned[1:] + turned[-1:]
        tiles = [
            jnp.where(chosen, jnp.where(inside, turned[i], after[i]), tiles[i])
            for i in range(span + 1)
        ]
        step //= 2
    for i in range(places):
        for j in range(span):
            staged[:, i * span + j, :] = tiles[j][i * peers : (i + 1) * peers]
    replies[...] = staged[...].astype(BF16)
    for j in range(peers - 1):
        answer(j, 0)
    keep_back = pltpu.make_async_copy(replies.at[0], answers.at[0], back_sem.at[2])
    keep_back.start()

    keep_back.wait()
    pltpu.make_async_copy(replies.at[others], answers.at[others], back_sem.at[1]).wait()
    stacked = dot(of_rows, answers[...].astype(F32).reshape(rows_all, LANES).astype(BF16))
    tops = [stacked[ROWS * j : ROWS * (j + 1)] for j in range(span)]
    square = tops[0] * tops[0]
    for top in tops[1:]:
        square = square + top * top
    mean = jnp.sum(square, axis=1, keepdims=True) * (1.0 / length)
    root = lax.rsqrt(mean + EPSILON)
    for j in range(span):
        out[:, j * LANES : (j + 1) * LANES] = tops[j] * root

    for k in range(len(ROUTES)):
        if k in relays:
            relay_copy(k).wait_send()
        for n in ROUTES[k][1]:
            if n:
                part_copy(k, n).wait_send()
                continue

            @pl.when(jnp.logical_not(stays(k)))
            def _():
                part_copy(k, n).wait_send()

    pltpu.make_async_copy(outbox.at[others], inbox.at[others], box_sem.at[0]).wait()
    pltpu.make_async_copy(replies.at[others], answers.at[others], back_sem.at[0]).wait()


def on_device(samples, templates, station_list, station_count, moveout, offsets):
    stations, channels, part = samples.shape
    tpl_dev, width, _, length = templates.shape
    tpl, sta = lax.axis_size("tpl"), lax.axis_size("sta")
    sizes = (tpl, sta, stations, channels, tpl_dev, width, length, part)
    held = stations * channels
    packs = -(-(held // ROWS) // (LANES // (part % LANES)))
    packed = part // LANES * held + ROWS * packs
    rows = jnp.transpose(samples, (1, 0, 2)).reshape(channels * stations, part)
    quads = jnp.transpose(templates, (1, 2, 0, 3)).reshape(width * channels, tpl_dev, length)
    offset_grid = offsets.reshape(-1, LANES)
    frame = 2 * length
    entries = tpl_dev * width * channels
    columns = (entries + LANES - 1) // LANES * LANES
    hbm = pl.BlockSpec(memory_space=pltpu.HBM)
    vmem = pl.BlockSpec(memory_space=pltpu.VMEM)
    dma = pltpu.SemaphoreType.DMA
    scaled = pl.pallas_call(
        functools.partial(kernel, sizes),
        out_shape=jax.ShapeDtypeStruct((ROWS, length), F32),
        in_specs=[hbm] * 9,
        out_specs=vmem,
        scratch_shapes=[
            pltpu.VMEM((frame, frame), BF16),
            pltpu.VMEM((frame, length), BF16),
            pltpu.VMEM((frame, length), BF16),
            pltpu.VMEM((width * channels, tpl_dev, length), BF16),
            pltpu.VMEM(station_list.shape, jnp.int32),
            pltpu.SMEM(station_count.shape, jnp.int32),
            pltpu.VMEM(moveout.shape, jnp.int32),
            pltpu.VMEM(offset_grid.shape, jnp.int32),
            pltpu.VMEM((columns // ROWS, ROWS, length), F32),
            pltpu.VMEM((4 * ROWS, LANES), F32),
            pltpu.VMEM((sta * ROWS, columns), BF16),
            pltpu.VMEM((held, part), BF16),
            pltpu.VMEM((packed, LANES), BF16),
            pltpu.VMEM((len(ROUTES), packed, LANES), BF16),
            pltpu.VMEM((sta // 2, BOX, length), BF16),
            pltpu.VMEM((sta // 2, BOX, length), BF16),
            pltpu.VMEM((2 * tpl, packed, LANES), BF16),
            pltpu.VMEM((sta // 2, BOX, LANES), F32),
            pltpu.VMEM((sta // 2, BOX, LANES), BF16),
            pltpu.VMEM((sta // 2, BOX, LANES), BF16),
            dma((9,)),
            dma((2 * tpl,)),
            dma((2 * tpl,)),
            dma((len(ROUTES),)),
            dma((len(ROUTES),)),
            dma((3,)),
            dma((3,)),
        ],
        compiler_params=pltpu.CompilerParams(
            collective_id=0, has_side_effects=True, vmem_limit_bytes=60 * 2**20
        ),
        cost_estimate=pl.CostEstimate(
            flops=2 * 10**9, bytes_accessed=6 * 10**6, transcendentals=10**5
        ),
    )(rows, quads, station_list, station_count, moveout, offset_grid, *tables(length))
    return scaled[:tpl_dev]


def solution(mesh):
    in_specs = (
        P("sta", None, "tpl"),
        P(("tpl", "sta"), None, None, None),
        P(("tpl", "sta"), None),
        P(("tpl", "sta")),
        P(("tpl", "sta"), None),
        P(),
    )
    out_specs = P(("tpl", "sta"), None)
    return jax.shard_map(
        on_device, mesh=mesh, in_specs=in_specs, out_specs=out_specs, check_vma=False
    )
```
